128 devices in a mesh: seq: 16 (over x_hi, z, core), head: 8 (over y, x_lo).
Axes of the slice: x: 4 (x_hi: 2, x_lo: 2; x = x_hi * 2 + x_lo), y: 4, z: 4, core: 2. Of those that a mesh axis runs over, the one named last changes fastest.
Arguments:
- prompt_query: bfloat16 [1024, 8192], P('seq', 'head'), may hold values from -16 to 16
- prompt_key: bfloat16 [1024, 1024], P('seq', 'head'), may hold values from -16 to 16
- prompt_value: bfloat16 [1024, 1024], P('seq', 'head'), may hold values from -6 to 6
- reply_query: bfloat16 [8192, 8192], P('seq', 'head'), may hold values from -16 to 16
- reply_key: bfloat16 [8192, 1024], P('seq', 'head'), may hold values from -6 to 6
- reply_value: bfloat16 [8192, 1024], P('seq', 'head'), may hold values from -6 to 6
- lengths: int32 [16], P('seq'), may hold values from 128 to 512, as said below
- out_weight: bfloat16 [8192, 5120], P('head', 'seq'), may hold values from -0.25 to 0.25
- prompt_grad: bfloat16 [1024, 5120], P('seq'), may hold values from -6 to 6
- reply_grad: bfloat16 [8192, 5120], P('seq'), may hold values from -6 to 6
Outputs:
- prompt_output: bfloat16 [1024, 5120], P('seq', 'head')
- reply_output: bfloat16 [8192, 5120], P('seq', 'head')
- prompt_query_grad: bfloat16 [1024, 8192], P('seq', 'head')
- prompt_key_grad: bfloat16 [1024, 1024], P('seq', 'head')
- prompt_value_grad: bfloat16 [1024, 1024], P('seq', 'head')
- reply_query_grad: bfloat16 [8192, 8192], P('seq', 'head')
- reply_key_grad: bfloat16 [8192, 1024], P('seq', 'head')
- reply_value_grad: bfloat16 [8192, 1024], P('seq', 'head')
The draws below stay inside these ranges and needn't reach their ends.
Inputs may be any that keep to these rules, and one draw needn't show every extreme that they name: `lengths`: multiples of 128; some response has 512 tokens and some 128.
All inputs are finite; a program needn't handle non-finite values.
Results may differ from the reference program's by a relative error of at most 0.029.
Values may be sent and summed in bfloat16 or wider, within the bound.
No kernel may reach another device: no remote copies, remote signals or barrier semaphores. Data moves between devices by JAX's collectives and lax.ppermute only.
A program may use at most 128 MiB of HBM per device.

```python
import jax
import jax.numpy as jnp
from jax import lax

D = 5120
HEADS = 64
KV_HEADS = 8
HEAD_DIM = 128
PROMPT_DEV = 64
REPLY_LEN = 512
LEN_STEP = 128
PROMPT = 1024
REPLIES = 16
N_SEQ = 16
N_HEAD = 8


def drawn_rows(key, count, width):
    return jnp.clip(jax.random.normal(key, (count, width), jnp.float32), -4.0, 4.0)


def draw_prompt_query(key, part):
    key = jax.random.fold_in(key, 11)
    rows = drawn_rows(key, PROMPT, HEADS * HEAD_DIM)
    return rows.astype(jnp.bfloat16)


def draw_prompt_key(key, part):
    key = jax.random.fold_in(key, 13)
    rows = drawn_rows(key, PROMPT, KV_HEADS * HEAD_DIM)
    return rows.astype(jnp.bfloat16)


def draw_reply_query(key, part):
    key = jax.random.fold_in(key, 17)
    rows = drawn_rows(key, REPLIES * REPLY_LEN, HEADS * HEAD_DIM)
    return rows.astype(jnp.bfloat16)


def draw_lengths(key, part):
    key = jax.random.fold_in(key, 5)
    first, second = jax.random.split(key)
    counts = jax.random.randint(first, (REPLIES,), 1, REPLY_LEN // LEN_STEP + 1, dtype=jnp.int32)
    order = jax.random.permutation(second, REPLIES)
    counts = counts.at[order[0]].set(REPLY_LEN // LEN_STEP).at[order[1]].set(1)
    return counts * LEN_STEP


def levels(rng, shape, cuts, low, largest):
    level, own = 1.0, jax.random.fold_in(rng, 6)
    for dim, shards_of in cuts:
        draws = jnp.exp(jax.random.uniform(jax.random.fold_in(own, dim), (shards_of,), jnp.float32, low / len(cuts), largest / len(cuts)))
        level = level * jnp.repeat(draws, shape[dim] // shards_of).reshape([-1 if axis == dim else 1 for axis in range(len(shape))])
    return level


def bell_draw(own_key, extent, deviation, most, cuts=(), kind=jnp.bfloat16):
    level = levels(own_key, extent, cuts, -0.22, 0.18) if cuts else 1.0
    result = jax.random.normal(own_key, extent, jnp.float32) * deviation * level
    return jnp.minimum(jnp.maximum(result, -most), most).astype(kind)


def setup_inputs(seed: int = 0) -> dict:
    streams_of = jax.random.split(jax.random.key(seed), 11)
    return {
        "prompt_query": draw_prompt_query(jax.random.fold_in(streams_of[10], 71), 0),
        "prompt_key": draw_prompt_key(jax.random.fold_in(streams_of[10], 71), 0),
        "prompt_value": bell_draw(streams_of[2], (PROMPT, KV_HEADS * HEAD_DIM), 1.0, 6.0, ((0, 16), (1, 8))),
        "reply_query": draw_reply_query(jax.random.fold_in(streams_of[10], 71), 0),
        "reply_key": bell_draw(streams_of[4], (REPLIES * REPLY_LEN, KV_HEADS * HEAD_DIM), 1.0, 6.0, ((0, 16), (1, 8))),
        "reply_value": bell_draw(streams_of[5], (REPLIES * REPLY_LEN, KV_HEADS * HEAD_DIM), 1.0, 6.0, ((0, 16), (1, 8))),
        "lengths": draw_lengths(jax.random.fold_in(streams_of[10], 71), 0),
        "out_weight": bell_draw(streams_of[7], (HEADS * HEAD_DIM, D), (HEAD_DIM * 4) ** -0.5, 0.25, ((0, 8), (1, 16))),
        "prompt_grad": bell_draw(streams_of[8], (PROMPT, D), 1.0, 6.0, ((0, 16),)),
        "reply_grad": bell_draw(streams_of[9], (REPLIES * REPLY_LEN, D), 1.0, 6.0, ((0, 16),)),
    }


def visible_keys(index, length, prompt_rows, reply_rows, prompt_len):
    row_ids = jnp.arange(prompt_rows + reply_rows, dtype=jnp.int32)
    column = jnp.arange(prompt_len + reply_rows, dtype=jnp.int32)
    prompt_row = row_ids < prompt_rows
    position = index * prompt_rows + row_ids
    offset = row_ids - prompt_rows
    prompt_col = column < prompt_len
    own_col = column - prompt_len
    allowed = jnp.where(prompt_row[:, None], prompt_col[None, :] & (column[None, :] <= position[:, None]), prompt_col[None, :] | (own_col[None, :] <= offset[:, None]))
    live = prompt_row | (offset < length)
    return allowed, live


def rounded(value):
    return lax.optimization_barrier(value.astype(jnp.bfloat16)).astype(jnp.float32)


def group_attention(queries, keys, values, grads, allowed, live):
    scale = HEAD_DIM ** -0.5
    query_float = queries.astype(jnp.float32)
    key_float = keys.astype(jnp.float32)
    value_float = values.astype(jnp.float32)
    grad_float = grads.astype(jnp.float32)
    scores = jnp.einsum("rgd,kd->grk", query_float, key_float) * scale
    scores = jnp.where(allowed[None], scores, -jnp.inf)
    highest = jnp.max(scores, axis=2, keepdims=True)
    raised = jnp.where(allowed[None], jnp.exp(scores - highest), 0.0)
    shares = raised / jnp.sum(raised, axis=2, keepdims=True)
    weights = rounded(shares)
    attended = jnp.einsum("grk,kd->rgd", weights, value_float)
    attended = jnp.where(live[:, None, None], attended, 0.0).astype(jnp.bfloat16)
    attended_float = lax.optimization_barrier(attended).astype(jnp.float32)
    delta = jnp.transpose(jnp.sum(grad_float * attended_float, axis=2))[:, :, None]
    weight_grad = jnp.einsum("rgd,kd->grk", grad_float, value_float)
    score_grad = rounded(shares * (weight_grad - delta))
    query_grad = (jnp.einsum("grk,kd->rgd", score_grad, key_float) * scale).astype(jnp.bfloat16)
    key_grad = jnp.einsum("grk,rgd->kd", score_grad, query_float) * scale
    value_grad = jnp.einsum("grk,rgd->kd", weights, grad_float)
    return attended, query_grad, key_grad, value_grad


def project(attended, out_weight):
    group_cols = HEADS * HEAD_DIM // N_HEAD

    def add_group(total, index):
        columns = lax.dynamic_slice_in_dim(attended, index * group_cols, group_cols, 1)
        part_rows = lax.dynamic_slice_in_dim(out_weight, index * group_cols, group_cols, 0)
        term = rounded(jnp.dot(columns, part_rows, preferred_element_type=jnp.float32))
        return total + term, None

    total, _ = lax.scan(add_group, jnp.zeros((attended.shape[0], D), jnp.float32), jnp.arange(N_HEAD, dtype=jnp.int32))
    return total.astype(jnp.bfloat16)


def reference(prompt_query, prompt_key, prompt_value, reply_query, reply_key, reply_value, lengths, out_weight, prompt_grad, reply_grad):
    group = HEADS // KV_HEADS
    head_cols = HEADS * HEAD_DIM
    kv_cols = KV_HEADS * HEAD_DIM
    rows = PROMPT_DEV + REPLY_LEN
    key_count = PROMPT + REPLY_LEN
    prompt_up = jnp.dot(prompt_grad, out_weight.T, preferred_element_type=jnp.float32).astype(jnp.bfloat16)
    reply_up = jnp.dot(reply_grad, out_weight.T, preferred_element_type=jnp.float32).astype(jnp.bfloat16)
    reply_live = (jnp.arange(REPLY_LEN, dtype=jnp.int32)[None, :] < lengths[:, None]).reshape(REPLIES * REPLY_LEN)
    reply_up = jnp.where(reply_live[:, None], reply_up, jnp.zeros((), reply_up.dtype))

    def one_device(index):
        queries = jnp.concatenate([lax.dynamic_slice_in_dim(prompt_query, index * PROMPT_DEV, PROMPT_DEV, 0), lax.dynamic_slice_in_dim(reply_query, index * REPLY_LEN, REPLY_LEN, 0)], 0)
        keys = jnp.concatenate([prompt_key, lax.dynamic_slice_in_dim(reply_key, index * REPLY_LEN, REPLY_LEN, 0)], 0)
        values = jnp.concatenate([prompt_value, lax.dynamic_slice_in_dim(reply_value, index * REPLY_LEN, REPLY_LEN, 0)], 0)
        grads = jnp.concatenate([lax.dynamic_slice_in_dim(prompt_up, index * PROMPT_DEV, PROMPT_DEV, 0), lax.dynamic_slice_in_dim(reply_up, index * REPLY_LEN, REPLY_LEN, 0)], 0)
        length = lax.dynamic_index_in_dim(lengths, index, 0, keepdims=False)
        allowed, live = visible_keys(index, length, PROMPT_DEV, REPLY_LEN, PROMPT)
        query_groups = queries.reshape(rows, KV_HEADS, group, HEAD_DIM).transpose(1, 0, 2, 3)
        grad_groups = grads.reshape(rows, KV_HEADS, group, HEAD_DIM).transpose(1, 0, 2, 3)
        key_groups = keys.reshape(key_count, KV_HEADS, HEAD_DIM).transpose(1, 0, 2)
        value_groups = values.reshape(key_count, KV_HEADS, HEAD_DIM).transpose(1, 0, 2)

        def one_group(item):
            return group_attention(item[0], item[1], item[2], item[3], allowed, live)

        attended, query_grad, key_grad, value_grad = lax.map(one_group, (query_groups, key_groups, value_groups, grad_groups))
        return (attended.transpose(1, 0, 2, 3).reshape(rows, head_cols), query_grad.transpose(1, 0, 2, 3).reshape(rows, head_cols), key_grad.transpose(1, 0, 2).reshape(key_count, kv_cols), value_grad.transpose(1, 0, 2).reshape(key_count, kv_cols))

    attended, query_grad, key_grad, value_grad = lax.map(one_device, jnp.arange(N_SEQ, dtype=jnp.int32))
    prompt_attended = attended[:, :PROMPT_DEV].reshape(PROMPT, head_cols)
    reply_attended = attended[:, PROMPT_DEV:].reshape(REPLIES * REPLY_LEN, head_cols)
    prompt_output = project(prompt_attended, out_weight)
    reply_output = project(reply_attended, out_weight)
    prompt_query_grad = query_grad[:, :PROMPT_DEV].reshape(PROMPT, head_cols)
    reply_query_grad = query_grad[:, PROMPT_DEV:].reshape(REPLIES * REPLY_LEN, head_cols)
    prompt_key_grad = jnp.sum(key_grad[:, :PROMPT], axis=0).astype(jnp.bfloat16)
    prompt_value_grad = jnp.sum(value_grad[:, :PROMPT], axis=0).astype(jnp.bfloat16)
    reply_key_grad = key_grad[:, PROMPT:].reshape(REPLIES * REPLY_LEN, kv_cols).astype(jnp.bfloat16)
    reply_value_grad = value_grad[:, PROMPT:].reshape(REPLIES * REPLY_LEN, kv_cols).astype(jnp.bfloat16)
    return (prompt_output, reply_output, prompt_query_grad, prompt_key_grad, prompt_value_grad, reply_query_grad, reply_key_grad, reply_value_grad)
```

```python
import jax
import jax.numpy as jnp
from jax import lax
from jax.experimental import pallas as pl
from jax.experimental.pallas import tpu as pltpu
from jax.sharding import PartitionSpec as P

DIM = 128
BF = jnp.bfloat16
F32 = jnp.float32
SCALE = DIM**-0.5
EXP_SCALE = SCALE * 1.4426950408889634
VMEM_LIMIT = 44 * 1024 * 1024


def dot_nn(a, b):
    return lax.dot_general(a, b, (((1,), (0,)), ((), ())), preferred_element_type=F32)


def dot_nt(a, b):
    return lax.dot_general(a, b, (((1,), (1,)), ((), ())), preferred_element_type=F32)


def forward_kernel(
    index_ref, length_ref, query_ref, prompt_query_ref, key_ref, value_ref, reply_key_ref, reply_value_ref,
    weight_ref, prompt_weight_ref, out_ref, prompt_out_ref, value_t, scores, stack,
):
    step = pl.program_id(0)
    heads = pl.num_programs(0) - 1
    prompt = key_ref.shape[0]
    rows = query_ref.shape[0]
    keys = prompt + rows
    prompt_rows = prompt_query_ref.shape[0]

    @pl.when(step == 0)
    def _():
        value_t[:, :prompt] = value_ref[...].T
        value_t[:, prompt:] = reply_value_ref[...].T

    @pl.when(step < heads)
    def _():
        query = query_ref[...]
        half = rows // 2
        scores[:prompt, :] = dot_nt(key_ref[...], query)
        scores[prompt : prompt + half, :] = dot_nt(reply_key_ref[:half], query)
        scores[prompt + half :, half:] = dot_nt(reply_key_ref[half:], query[half:])
        seen = lax.broadcasted_iota(jnp.int32, (DIM, DIM), 0) <= lax.broadcasted_iota(jnp.int32, (DIM, DIM), 1)
        for tile in range(rows // DIM):
            lanes = slice(tile * DIM, (tile + 1) * DIM)
            full = prompt + tile * DIM
            wide = scores[:full, lanes]
            diag = jnp.where(seen, scores[full : full + DIM, lanes], -jnp.inf)
            top = jnp.maximum(jnp.max(wide, axis=0, keepdims=True), jnp.max(diag, axis=0, keepdims=True))
            wide = jnp.exp2((wide - top) * EXP_SCALE)
            diag = jnp.exp2((diag - top) * EXP_SCALE)
            total = jnp.sum(wide, axis=0, keepdims=True) + jnp.sum(diag, axis=0, keepdims=True)
            inverse = 1.0 / total
            weight_ref[0, :full, lanes] = (wide * inverse).astype(BF)
            weight_ref[0, full : full + DIM, lanes] = (diag * inverse).astype(BF)
            if full + DIM < keys:
                weight_ref[0, full + DIM :, lanes] = jnp.zeros((keys - full - DIM, DIM), BF)
        out = dot_nn(value_t[...], weight_ref[0]).T
        live = lax.broadcasted_iota(jnp.int32, (rows, DIM), 0) < length_ref[0]
        out_ref[...] = jnp.where(live, out, 0.0).astype(BF)

    @pl.when(step == heads)
    def _():
        for head in range(rows // prompt_rows):
            stack[head * prompt_rows : (head + 1) * prompt_rows, :] = prompt_query_ref[:, head * DIM : (head + 1) * DIM]
        scores[:prompt, :] = dot_nt(key_ref[...], stack[...])
        first = index_ref[0] * prompt_rows
        for tile in range(rows // DIM):
            lanes = slice(tile * DIM, (tile + 1) * DIM)
            place = lax.broadcasted_iota(jnp.int32, (prompt, DIM), 1) % prompt_rows + first
            seen = lax.broadcasted_iota(jnp.int32, (prompt, DIM), 0) <= place
            part = jnp.where(seen, scores[:prompt, lanes], -jnp.inf)
            top = jnp.max(part, axis=0, keepdims=True)
            part = jnp.exp2((part - top) * EXP_SCALE)
            inverse = 1.0 / jnp.sum(part, axis=0, keepdims=True)
            prompt_weight_ref[:, lanes] = (part * inverse).astype(BF)
        out = dot_nn(value_t[:, :prompt], prompt_weight_ref[...]).T.astype(BF)
        for head in range(rows // prompt_rows):
            prompt_out_ref[:, head * DIM : (head + 1) * DIM] = out[head * prompt_rows : (head + 1) * prompt_rows, :]


def attention_forward(index, length, reply_query, prompt_query, kv, reply_key, reply_value):
    rows, columns = reply_query.shape
    prompt_rows = prompt_query.shape[0]
    heads = columns // DIM
    prompt = kv.shape[0]
    keys = prompt + rows
    last = heads - 1
    whole = lambda shape: pl.BlockSpec(shape, lambda g: (0, 0))
    return pl.pallas_call(
        forward_kernel,
        grid=(heads + 1,),
        in_specs=[
            pl.BlockSpec(memory_space=pltpu.SMEM),
            pl.BlockSpec(memory_space=pltpu.SMEM),
            pl.BlockSpec((rows, DIM), lambda g: (0, jnp.minimum(g, last))),
            whole((prompt_rows, columns)),
            pl.BlockSpec((prompt, DIM), lambda g: (0, 0)),
            pl.BlockSpec((prompt, DIM), lambda g: (0, 1)),
            whole((rows, DIM)),
            whole((rows, DIM)),
        ],
        out_specs=[
            pl.BlockSpec((1, keys, rows), lambda g: (jnp.minimum(g, last), 0, 0)),
            whole((prompt, rows)),
            pl.BlockSpec((rows, DIM), lambda g: (0, jnp.minimum(g, last))),
            whole((prompt_rows, columns)),
        ],
        out_shape=[
            jax.ShapeDtypeStruct((heads, keys, rows), BF),
            jax.ShapeDtypeStruct((prompt, rows), BF),
            jax.ShapeDtypeStruct((rows, columns), BF),
            jax.ShapeDtypeStruct((prompt_rows, columns), BF),
        ],
        scratch_shapes=[
            pltpu.VMEM((DIM, keys), BF),
            pltpu.VMEM((keys, rows), F32),
            pltpu.VMEM((rows, DIM), BF),
        ],
        compiler_params=pltpu.CompilerParams(vmem_limit_bytes=VMEM_LIMIT),
        cost_estimate=pl.CostEstimate(flops=4 * heads * keys * rows * DIM, bytes_accessed=18 * 2**20, transcendentals=heads * keys * rows),
        name="attention_forward",
    )(index, length, reply_query, prompt_query, kv, kv, reply_key, reply_value)


def backward_kernel(
    weight_ref, prompt_weight_ref, query_ref, grad_ref, out_ref, prompt_query_ref, prompt_grad_ref, prompt_out_ref,
    key_ref, value_ref, reply_key_ref, reply_value_ref,
    query_grad_ref, prompt_query_grad_ref, kv_grad_ref, reply_key_grad_ref, reply_value_grad_ref,
    key_t, score_grad, key_grad, value_grad, stack,
):
    step = pl.program_id(0)
    heads = pl.num_programs(0) - 1
    prompt = key_ref.shape[0]
    rows = query_ref.shape[0]
    keys = prompt + rows
    half = rows // 2
    prompt_rows = prompt_query_ref.shape[0]

    @pl.when(step == 0)
    def _():
        key_t[:, :prompt] = key_ref[...].T
        key_t[:, prompt:] = reply_key_ref[...].T
        key_grad[...] = jnp.zeros_like(key_grad)
        value_grad[...] = jnp.zeros_like(value_grad)
        score_grad[prompt + half :, :half] = jnp.zeros((half, half), BF)

    def row_delta(grad, out):
        return jnp.sum((grad.astype(F32) * out.astype(F32)).T, axis=0, keepdims=True)

    def key_block(weight, value, grad, query, delta, start, size, low):
        block = slice(start, start + size)
        slope = dot_nt(value, grad)
        part = (weight.astype(F32) * (slope - delta)).astype(BF)
        score_grad[block, low:] = part
        key_grad[block, :] += dot_nn(part, query)
        value_grad[block, :] += dot_nn(weight, grad)

    @pl.when(step < heads)
    def _():
        query, grad = query_ref[...], grad_ref[...]
        delta = row_delta(grad, out_ref[...])
        for start in range(0, prompt, 256):
            key_block(weight_ref[0, start : start + 256, :], value_ref[start : start + 256, :], grad, query, delta, start, 256, 0)
        key_block(weight_ref[0, prompt : prompt + half, :], reply_value_ref[:half], grad, query, delta, prompt, half, 0)
        key_block(
            weight_ref[0, prompt + half :, half:], reply_value_ref[half:], grad[half:], query[half:], delta[:, half:], prompt + half, half, half
        )
        query_grad_ref[...] = (dot_nn(key_t[...], score_grad[...]).T * SCALE).astype(BF)

    @pl.when(step == heads)
    def _():
        count = rows // prompt_rows
        for head in range(count):
            place, lanes = slice(head * prompt_rows, (head + 1) * prompt_rows), slice(head * DIM, (head + 1) * DIM)
            stack[0, place, :] = prompt_query_ref[:, lanes]
            stack[1, place, :] = prompt_grad_ref[:, lanes]
            stack[2, place, :] = prompt_out_ref[:, lanes]
        query, grad = stack[0], stack[1]
        delta = row_delta(grad, stack[2])
        for start in range(0, prompt, 256):
            key_block(prompt_weight_ref[start : start + 256, :], value_ref[start : start + 256, :], grad, query, delta, start, 256, 0)
        result = (dot_nn(key_t[:, :prompt], score_grad[:prompt, :]).T * SCALE).astype(BF)
        for head in range(count):
            prompt_query_grad_ref[:, head * DIM : (head + 1) * DIM] = result[head * prompt_rows : (head + 1) * prompt_rows, :]
        kv_grad_ref[:, :DIM] = (key_grad[:prompt, :] * SCALE).astype(BF)
        kv_grad_ref[:, DIM:] = value_grad[:prompt, :].astype(BF)
        reply_key_grad_ref[...] = (key_grad[prompt:, :] * SCALE).astype(BF)
        reply_value_grad_ref[...] = value_grad[prompt:, :].astype(BF)


def attention_backward(weights, prompt_weights, reply_query, reply_up, reply_att, prompt_query, prompt_up, prompt_att, kv, reply_key, reply_value):
    rows, columns = reply_query.shape
    prompt_rows = prompt_query.shape[0]
    heads = columns // DIM
    prompt = kv.shape[0]
    keys = prompt + rows
    last = heads - 1
    whole = lambda shape: pl.BlockSpec(shape, lambda g: (0, 0))
    column = pl.BlockSpec((rows, DIM), lambda g: (0, jnp.minimum(g, last)))
    return pl.pallas_call(
        backward_kernel,
        grid=(heads + 1,),
        in_specs=[
            pl.BlockSpec((1, keys, rows), lambda g: (jnp.minimum(g, last), 0, 0)),
            whole((prompt, rows)),
            column,
            column,
            column,
            whole((prompt_rows, columns)),
            whole((prompt_rows, columns)),
            whole((prompt_rows, columns)),
            pl.BlockSpec((prompt, DIM), lambda g: (0, 0)),
            pl.BlockSpec((prompt, DIM), lambda g: (0, 1)),
            whole((rows, DIM)),
            whole((rows, DIM)),
        ],
        out_specs=[
            column,
            whole((prompt_rows, columns)),
            whole((prompt, 2 * DIM)),
            whole((rows, DIM)),
            whole((rows, DIM)),
        ],
        out_shape=[
            jax.ShapeDtypeStruct((rows, columns), BF),
            jax.ShapeDtypeStruct((prompt_rows, columns), BF),
            jax.ShapeDtypeStruct((prompt, 2 * DIM), BF),
            jax.ShapeDtypeStruct((rows, DIM), BF),
            jax.ShapeDtypeStruct((rows, DIM), BF),
        ],
        scratch_shapes=[
            pltpu.VMEM((DIM, keys), BF),
            pltpu.VMEM((keys, rows), BF),
            pltpu.VMEM((keys, DIM), F32),
            pltpu.VMEM((keys, DIM), F32),
            pltpu.VMEM((3, rows, DIM), BF),
        ],
        compiler_params=pltpu.CompilerParams(vmem_limit_bytes=VMEM_LIMIT),
        cost_estimate=pl.CostEstimate(flops=8 * heads * keys * rows * DIM, bytes_accessed=18 * 2**20, transcendentals=0),
        name="attention_backward",
    )(weights, prompt_weights, reply_query, reply_up, reply_att, prompt_query, prompt_up, prompt_att, kv, kv, reply_key, reply_value)


def body(prompt_query, prompt_key, prompt_value, reply_query, reply_key, reply_value, lengths, out_weight, prompt_grad, reply_grad):
    prompt_rows = prompt_query.shape[0]
    reply_rows = reply_query.shape[0]
    n_seq, n_head = lax.axis_size("seq"), lax.axis_size("head")
    seq, head = lax.axis_index("seq"), lax.axis_index("head")
    weight = lax.all_gather(out_weight.T, "seq", axis=0, tiled=True)
    own = jnp.concatenate([prompt_key, prompt_value], 1)
    kv = lax.all_to_all(jnp.broadcast_to(own[None], (n_seq,) + own.shape), "seq", 0, 0).reshape(n_seq * prompt_rows, 2 * DIM)
    weights, prompt_weights, reply_att, prompt_att = attention_forward(
        seq.reshape(1).astype(jnp.int32), lengths, reply_query, prompt_query, kv, reply_key, reply_value
    )
    attended = jnp.concatenate([prompt_att, reply_att], 0)
    width = weight.shape[0] // n_head
    mixed = None
    for hop in [7, 6, 5, 4, 3, 2, 1, 0]:
        target = head ^ hop
        block = lax.dynamic_slice_in_dim(weight, target * width, width, 0)
        term = dot_nt(attended, block).astype(BF)
        if hop:
            term = lax.ppermute(term, "head", [(i, i ^ hop) for i in range(n_head)])
        mixed = term.astype(F32) if mixed is None else mixed + term.astype(F32)
    mixed = mixed.astype(BF)
    prompt_up = dot_nn(prompt_grad, weight).astype(BF)
    live = jnp.arange(reply_rows, dtype=jnp.int32) < lengths[0]
    reply_up = jnp.where(live[:, None], dot_nn(reply_grad, weight).astype(BF), jnp.zeros((), BF))
    query_grad, prompt_query_grad, kv_grad, reply_key_grad, reply_value_grad = attention_backward(
        weights, prompt_weights, reply_query, reply_up, reply_att, prompt_query, prompt_up, prompt_att, kv, reply_key, reply_value
    )
    terms = lax.all_to_all(kv_grad.reshape(n_seq, prompt_rows, 2 * DIM), "seq", 0, 0)
    kv_total = jnp.sum(terms.astype(F32), axis=0).astype(BF)
    return (
        mixed[:prompt_rows],
        mixed[prompt_rows:],
        prompt_query_grad,
        kv_total[:, :DIM],
        kv_total[:, DIM:],
        query_grad,
        reply_key_grad,
        reply_value_grad,
    )


def solution(mesh):
    cut = P("seq", "head")
    in_specs = (cut, cut, cut, cut, cut, cut, P("seq"), P("head", "seq"), P("seq", None), P("seq", None))
    return jax.shard_map(body, mesh=mesh, in_specs=in_specs, out_specs=(cut,) * 8, check_vma=False)
```

```python
import jax
import jax.numpy as jnp
from jax import lax
from jax.experimental import pallas as pl
from jax.experimental.pallas import tpu as pltpu
from jax.sharding import PartitionSpec as P

DIM = 128
BF = jnp.bfloat16
F32 = jnp.float32
SCALE = DIM**-0.5
EXP_SCALE = SCALE * 1.4426950408889634
VMEM_LIMIT = 60 * 1024 * 1024


def dot_nn(a, b):
    return lax.dot_general(a, b, (((1,), (0,)), ((), ())), preferred_element_type=F32)


def dot_nt(a, b):
    return lax.dot_general(a, b, (((1,), (1,)), ((), ())), preferred_element_type=F32)


def forward_kernel(
    index_ref, length_ref, query_ref, prompt_query_ref, key_ref, value_ref, reply_key_ref, reply_value_ref,
    weight_ref, prompt_weight_ref, out_ref, prompt_out_ref, value_t, scores, stack,
):
    step = pl.program_id(0)
    heads = pl.num_programs(0) - 1
    prompt = key_ref.shape[0]
    rows = query_ref.shape[0]
    keys = prompt + rows
    prompt_rows = prompt_query_ref.shape[0]

    @pl.when(step == 0)
    def _():
        value_t[:, :prompt] = value_ref[...].T
        value_t[:, prompt:] = reply_value_ref[...].T

    @pl.when(step < heads)
    def _():
        query = query_ref[...]
        half = rows // 2
        scores[:prompt, :] = dot_nt(key_ref[...], query)
        scores[prompt : prompt + half, :] = dot_nt(reply_key_ref[:half], query)
        scores[prompt + half :, half:] = dot_nt(reply_key_ref[half:], query[half:])
        seen = lax.broadcasted_iota(jnp.int32, (DIM, DIM), 0) <= lax.broadcasted_iota(jnp.int32, (DIM, DIM), 1)
        for tile in range(rows // DIM):
            lanes = slice(tile * DIM, (tile + 1) * DIM)
            full = prompt + tile * DIM
            wide = scores[:full, lanes]
            diag = jnp.where(seen, scores[full : full + DIM, lanes], -jnp.inf)
            top = jnp.maximum(jnp.max(wide, axis=0, keepdims=True), jnp.max(diag, axis=0, keepdims=True))
            wide = jnp.exp2((wide - top) * EXP_SCALE)
            diag = jnp.exp2((diag - top) * EXP_SCALE)
            total = jnp.sum(wide, axis=0, keepdims=True) + jnp.sum(diag, axis=0, keepdims=True)
            inverse = 1.0 / total
            weight_ref[0, :full, lanes] = (wide * inverse).astype(BF)
            weight_ref[0, full : full + DIM, lanes] = (diag * inverse).astype(BF)
            if full + DIM < keys:
                weight_ref[0, full + DIM :, lanes] = jnp.zeros((keys - full - DIM, DIM), BF)
        out = dot_nn(value_t[...], weight_ref[0]).T
        live = lax.broadcasted_iota(jnp.int32, (rows, DIM), 0) < length_ref[0]
        out_ref[...] = jnp.where(live, out, 0.0).astype(BF)

    @pl.when(step == heads)
    def _():
        for head in range(rows // prompt_rows):
            stack[head * prompt_rows : (head + 1) * prompt_rows, :] = prompt_query_ref[:, head * DIM : (head + 1) * DIM]
        scores[:prompt, :] = dot_nt(key_ref[...], stack[...])
        first = index_ref[0] * prompt_rows
        for tile in range(rows // DIM):
            lanes = slice(tile * DIM, (tile + 1) * DIM)
            place = lax.broadcasted_iota(jnp.int32, (prompt, DIM), 1) % prompt_rows + first
            seen = lax.broadcasted_iota(jnp.int32, (prompt, DIM), 0) <= place
            part = jnp.where(seen, scores[:prompt, lanes], -jnp.inf)
            top = jnp.max(part, axis=0, keepdims=True)
            part = jnp.exp2((part - top) * EXP_SCALE)
            inverse = 1.0 / jnp.sum(part, axis=0, keepdims=True)
            prompt_weight_ref[:, lanes] = (part * inverse).astype(BF)
        out = dot_nn(value_t[:, :prompt], prompt_weight_ref[...]).T.astype(BF)
        for head in range(rows // prompt_rows):
            prompt_out_ref[:, head * DIM : (head + 1) * DIM] = out[head * prompt_rows : (head + 1) * prompt_rows, :]


def attention_forward(index, length, reply_query, prompt_query, kv, reply_key, reply_value):
    rows, columns = reply_query.shape
    prompt_rows = prompt_query.shape[0]
    heads = columns // DIM
    prompt = kv.shape[0]
    keys = prompt + rows
    last = heads - 1
    whole = lambda shape: pl.BlockSpec(shape, lambda g: (0, 0))
    return pl.pallas_call(
        forward_kernel,
        grid=(heads + 1,),
        in_specs=[
            pl.BlockSpec(memory_space=pltpu.SMEM),
            pl.BlockSpec(memory_space=pltpu.SMEM),
            pl.BlockSpec((rows, DIM), lambda g: (0, jnp.minimum(g, last))),
            whole((prompt_rows, columns)),
            pl.BlockSpec((prompt, DIM), lambda g: (0, 0)),
            pl.BlockSpec((prompt, DIM), lambda g: (0, 1)),
            whole((rows, DIM)),
            whole((rows, DIM)),
        ],
        out_specs=[
            pl.BlockSpec((1, keys, rows), lambda g: (jnp.minimum(g, last), 0, 0)),
            whole((prompt, rows)),
            pl.BlockSpec((rows, DIM), lambda g: (0, jnp.minimum(g, last))),
            whole((prompt_rows, columns)),
        ],
        out_shape=[
            jax.ShapeDtypeStruct((heads, keys, rows), BF),
            jax.ShapeDtypeStruct((prompt, rows), BF),
            jax.ShapeDtypeStruct((rows, columns), BF),
            jax.ShapeDtypeStruct((prompt_rows, columns), BF),
        ],
        scratch_shapes=[
            pltpu.VMEM((DIM, keys), BF),
            pltpu.VMEM((keys, rows), F32),
            pltpu.VMEM((rows, DIM), BF),
        ],
        compiler_params=pltpu.CompilerParams(vmem_limit_bytes=VMEM_LIMIT),
        cost_estimate=pl.CostEstimate(flops=4 * heads * keys * rows * DIM, bytes_accessed=18 * 2**20, transcendentals=heads * keys * rows),
        name="attention_forward",
    )(index, length, reply_query, prompt_query, kv, kv, reply_key, reply_value)


def backward_kernel(
    weight_ref, prompt_weight_ref, query_ref, grad_ref, out_ref, prompt_query_ref, prompt_grad_ref, prompt_out_ref,
    key_ref, value_ref, reply_key_ref, reply_value_ref,
    query_grad_ref, prompt_query_grad_ref, kv_grad_ref, reply_key_grad_ref, reply_value_grad_ref,
    key_t, score_grad, key_grad, value_grad, stack,
):
    step = pl.program_id(0)
    heads = pl.num_programs(0) - 1
    prompt = key_ref.shape[0]
    rows = query_ref.shape[0]
    keys = prompt + rows
    half = rows // 2
    prompt_rows = prompt_query_ref.shape[0]

    @pl.when(step == 0)
    def _():
        key_t[:, :prompt] = key_ref[...].T
        key_t[:, prompt:] = reply_key_ref[...].T
        key_grad[...] = jnp.zeros_like(key_grad)
        value_grad[...] = jnp.zeros_like(value_grad)
        score_grad[prompt + half :, :half] = jnp.zeros((half, half), BF)

    def row_delta(grad, out):
        return jnp.sum((grad.astype(F32) * out.astype(F32)).T, axis=0, keepdims=True)

    def key_block(weight, value, grad, query, delta, start, size, low):
        block = slice(start, start + size)
        slope = dot_nt(value, grad)
        part = (weight.astype(F32) * (slope - delta)).astype(BF)
        score_grad[block, low:] = part
        key_grad[block, :] += dot_nn(part, query)
        value_grad[block, :] += dot_nn(weight, grad)

    @pl.when(step < heads)
    def _():
        query, grad = query_ref[...], grad_ref[...]
        delta = row_delta(grad, out_ref[...])
        for start in range(0, prompt, 256):
            key_block(weight_ref[0, start : start + 256, :], value_ref[start : start + 256, :], grad, query, delta, start, 256, 0)
        key_block(weight_ref[0, prompt : prompt + half, :], reply_value_ref[:half], grad, query, delta, prompt, half, 0)
        key_block(
            weight_ref[0, prompt + half :, half:], reply_value_ref[half:], grad[half:], query[half:], delta[:, half:], prompt + half, half, half
        )
        query_grad_ref[...] = (dot_nn(key_t[...], score_grad[...]).T * SCALE).astype(BF)

    @pl.when(step == heads)
    def _():
        count = rows // prompt_rows
        for head in range(count):
            place, lanes = slice(head * prompt_rows, (head + 1) * prompt_rows), slice(head * DIM, (head + 1) * DIM)
            stack[0, place, :] = prompt_query_ref[:, lanes]
            stack[1, place, :] = prompt_grad_ref[:, lanes]
            stack[2, place, :] = prompt_out_ref[:, lanes]
        query, grad = stack[0], stack[1]
        delta = row_delta(grad, stack[2])
        for start in range(0, prompt, 256):
            key_block(prompt_weight_ref[start : start + 256, :], value_ref[start : start + 256, :], grad, query, delta, start, 256, 0)
        result = (dot_nn(key_t[:, :prompt], score_grad[:prompt, :]).T * SCALE).astype(BF)
        for head in range(count):
            prompt_query_grad_ref[:, head * DIM : (head + 1) * DIM] = result[head * prompt_rows : (head + 1) * prompt_rows, :]
        kv_grad_ref[:, :DIM] = (key_grad[:prompt, :] * SCALE).astype(BF)
        kv_grad_ref[:, DIM:] = value_grad[:prompt, :].astype(BF)
        reply_key_grad_ref[...] = (key_grad[prompt:, :] * SCALE).astype(BF)
        reply_value_grad_ref[...] = value_grad[prompt:, :].astype(BF)


def attention_backward(weights, prompt_weights, reply_query, reply_up, reply_att, prompt_query, prompt_up, prompt_att, kv, reply_key, reply_value):
    rows, columns = reply_query.shape
    prompt_rows = prompt_query.shape[0]
    heads = columns // DIM
    prompt = kv.shape[0]
    keys = prompt + rows
    last = heads - 1
    whole = lambda shape: pl.BlockSpec(shape, lambda g: (0, 0))
    column = pl.BlockSpec((rows, DIM), lambda g: (0, jnp.minimum(g, last)))
    return pl.pallas_call(
        backward_kernel,
        grid=(heads + 1,),
        in_specs=[
            pl.BlockSpec((1, keys, rows), lambda g: (jnp.minimum(g, last), 0, 0)),
            whole((prompt, rows)),
            column,
            column,
            column,
            whole((prompt_rows, columns)),
            whole((prompt_rows, columns)),
            whole((prompt_rows, columns)),
            pl.BlockSpec((prompt, DIM), lambda g: (0, 0)),
            pl.BlockSpec((prompt, DIM), lambda g: (0, 1)),
            whole((rows, DIM)),
            whole((rows, DIM)),
        ],
        out_specs=[
            column,
            whole((prompt_rows, columns)),
            whole((prompt, 2 * DIM)),
            whole((rows, DIM)),
            whole((rows, DIM)),
        ],
        out_shape=[
            jax.ShapeDtypeStruct((rows, columns), BF),
            jax.ShapeDtypeStruct((prompt_rows, columns), BF),
            jax.ShapeDtypeStruct((prompt, 2 * DIM), BF),
            jax.ShapeDtypeStruct((rows, DIM), BF),
            jax.ShapeDtypeStruct((rows, DIM), BF),
        ],
        scratch_shapes=[
            pltpu.VMEM((DIM, keys), BF),
            pltpu.VMEM((keys, rows), BF),
            pltpu.VMEM((keys, DIM), F32),
            pltpu.VMEM((keys, DIM), F32),
            pltpu.VMEM((3, rows, DIM), BF),
        ],
        compiler_params=pltpu.CompilerParams(vmem_limit_bytes=VMEM_LIMIT),
        cost_estimate=pl.CostEstimate(flops=8 * heads * keys * rows * DIM, bytes_accessed=18 * 2**20, transcendentals=0),
        name="attention_backward",
    )(weights, prompt_weights, reply_query, reply_up, reply_att, prompt_query, prompt_up, prompt_att, kv, kv, reply_key, reply_value)


def half_copies(chunks, order_ref, core_ref, gathered, sems):
    size = chunks[0].shape[0]
    core = core_ref[0]
    copies = []
    for slot in range(4):
        for side in range(2):
            place = order_ref[slot if side == 0 else SWAPPED[slot]]
            row = place * (2 * size) + (core if side == 0 else 1 - core) * size
            copies.append(
                pltpu.make_async_copy(
                    chunks[side * 4 + slot],
                    gathered.at[pl.ds(pl.multiple_of(row, size), size), :],
                    sems.at[place, side],
                )
            )
    return copies


def products_kernel(order_ref, core_ref, head_ref, half_ref, *refs):
    chunks = refs[:8]
    prompt_ref, reply_ref = refs[8:10]
    outs, (gathered, rows, held, sems, out_sems) = refs[-11:-5], refs[-5:]
    size = chunks[0].shape[0]
    for copy in half_copies(chunks, order_ref, core_ref, gathered, sems):
        copy.start()
    count = prompt_ref.shape[0]
    half = rows.shape[0] // 2
    rows[:count, :] = prompt_ref[...]
    rows[count:, :] = reply_ref[...]
    across, along = head_ref[0] % 2, head_ref[0] // 2

    def flush(slot, dy, dx):
        upper = [
            pltpu.make_async_copy(held.at[slot, pl.ds(0, half), :], outs[side].at[dy], out_sems.at[slot, 0]) for side in range(2)
        ]
        lower = [
            pltpu.make_async_copy(held.at[slot, pl.ds(half, half), :], outs[2 + turn].at[dx], out_sems.at[slot, 1]) for turn in range(4)
        ]
        return upper, lower

    for place in range(4):
        slot = place % 2
        if place >= 2:
            upper, lower = flush(slot, 0, 0)
            upper[0].wait()
            lower[0].wait()
        for side in range(2):
            pltpu.make_async_copy(chunks[side * 4], gathered.at[pl.ds(0, size), :], sems.at[place, side]).wait()
        block = gathered[2 * size * place : 2 * size * (place + 1), :]
        held[slot] = dot_nt(rows[...], block).astype(BF)
        target = half_ref[0] * 4 + place
        dy, dx = (target // 2 - along + 4) % 4, (target % 2 - across + 2) % 2
        upper, lower = flush(slot, dy, dx)
        for side in range(2):
            pl.when(dx == side)(upper[side].start)
        for turn in range(4):
            pl.when(dy == turn)(lower[turn].start)
    for slot in range(2):
        upper, lower = flush(slot, 0, 0)
        upper[0].wait()
        lower[0].wait()


def head_products(order, core, head, half, chunks, prompt_att, reply_att, earlier):
    total = prompt_att.shape[0] + reply_att.shape[0]
    size, depth = chunks[0].shape
    width = 2 * size
    anywhere = pl.BlockSpec(memory_space=pl.ANY)
    scalar = pl.BlockSpec(memory_space=pltpu.SMEM)
    return pl.pallas_call(
        products_kernel,
        in_specs=[scalar] * 4 + [anywhere] * 8 + [pl.BlockSpec(memory_space=pltpu.VMEM)] * 2 + [anywhere] * len(earlier),
        out_specs=[anywhere] * 6,
        out_shape=[jax.ShapeDtypeStruct((4, total // 2, width), BF)] * 2 + [jax.ShapeDtypeStruct((2, total // 2, width), BF)] * 4,
        input_output_aliases={14 + place: place for place in range(len(earlier))},
        scratch_shapes=[
            pltpu.VMEM((8 * size, depth), BF),
            pltpu.VMEM((total, depth), BF),
            pltpu.VMEM((2, total, width), BF),
            pltpu.SemaphoreType.DMA((4, 2)),
            pltpu.SemaphoreType.DMA((2, 2)),
        ],
        compiler_params=pltpu.CompilerParams(vmem_limit_bytes=VMEM_LIMIT),
        cost_estimate=pl.CostEstimate(flops=2 * total * depth * 8 * size, bytes_accessed=9 * 2**20, transcendentals=0),
        name="head_products",
    )(order, core, head, half, *chunks, prompt_att, reply_att, *earlier)


def upstream_kernel(order_ref, core_ref, half_ref, length_ref, *refs):
    chunks = refs[:8]
    prompt_ref, reply_ref = refs[8:10]
    last = len(refs) == 17
    earlier, outs, (gathered, rows, sems, row_sems) = (refs[10:11], refs[11:13], refs[13:]) if last else ((), refs[10:11], refs[11:])
    step = pl.program_id(0)
    count = prompt_ref.shape[0]

    @pl.when(step == 0)
    def _():
        columns = pl.ds(pl.multiple_of(half_ref[0] * rows.shape[1], rows.shape[1]), rows.shape[1])
        copies = half_copies(chunks, order_ref, core_ref, gathered, sems)
        copies.append(pltpu.make_async_copy(prompt_ref.at[:, columns], rows.at[pl.ds(0, count), :], row_sems.at[0]))
        copies.append(pltpu.make_async_copy(reply_ref.at[:, columns], rows.at[pl.ds(count, rows.shape[0] - count), :], row_sems.at[1]))
        for copy in copies:
            copy.start()
        for copy in copies:
            copy.wait()

    width = outs[0].shape[1]
    total = dot_nn(rows[...], gathered[:, pl.ds(pl.multiple_of(step * width, width), width)])
    if not last:
        outs[0][...] = total
    else:
        total = total + earlier[0][...]
        outs[0][...] = total[:count].astype(BF)
        live = lax.broadcasted_iota(jnp.int32, (total.shape[0] - count, width), 0) < length_ref[0]
        outs[1][...] = jnp.where(live, total[count:], 0.0).astype(BF)


def upstream(order, core, half, lengths, chunks, prompt_grad, reply_grad, earlier):
    size, depth = chunks[0].shape
    prompt_rows, reply_rows = prompt_grad.shape[0], reply_grad.shape[0]
    total = prompt_rows + reply_rows
    parts = 2
    anywhere = pl.BlockSpec(memory_space=pl.ANY)
    scalar = pl.BlockSpec(memory_space=pltpu.SMEM)
    column = lambda rows: pl.BlockSpec((rows, depth // parts), lambda k: (0, k))
    if earlier is None:
        out_specs, out_shape = [column(total)], [jax.ShapeDtypeStruct((total, depth), F32)]
    else:
        out_specs = [column(prompt_rows), column(reply_rows)]
        out_shape = [jax.ShapeDtypeStruct((prompt_rows, depth), BF), jax.ShapeDtypeStruct((reply_rows, depth), BF)]
    return pl.pallas_call(
        upstream_kernel,
        grid=(parts,),
        in_specs=[scalar] * 4 + [anywhere] * 10 + ([] if earlier is None else [column(total)]),
        out_specs=out_specs,
        out_shape=out_shape,
        scratch_shapes=[
            pltpu.VMEM((8 * size, depth), BF),
            pltpu.VMEM((total, 8 * size), BF),
            pltpu.SemaphoreType.DMA((4, 2)),
            pltpu.SemaphoreType.DMA((2,)),
        ],
        compiler_params=pltpu.CompilerParams(vmem_limit_bytes=VMEM_LIMIT),
        cost_estimate=pl.CostEstimate(flops=2 * total * depth * 8 * size, bytes_accessed=9 * 2**20, transcendentals=0),
        name="upstream",
    )(order, core, half, lengths, *chunks, prompt_grad, reply_grad, *([] if earlier is None else [earlier]))


SWAPPED = (0, 2, 1, 3)


def seq_perm(move):
    pairs = []
    for x in range(2):
        for z in range(4):
            for core in range(2):
                to_x, to_z, to_core = move(x, z, core)
                pairs.append((x * 8 + z * 2 + core, (to_x % 2) * 8 + (to_z % 4) * 2 + to_core % 2))
    return pairs


ALONG = seq_perm(lambda x, z, core: (x, z + 1 - 2 * core, core))
AGAINST = seq_perm(lambda x, z, core: (x, z - 1 + 2 * core, core))
PEER = seq_perm(lambda x, z, core: (x + 1, z, core))
SIBLING = seq_perm(lambda x, z, core: (x, z, core + 1))


def head_perm(dy, dx):
    return [(y * 2 + x, ((y + dy) % 4) * 2 + (x + dx) % 2) for y in range(4) for x in range(2)]


def gather_first(own):
    return [own] + [lax.ppermute(own, "seq", perm) for perm in (ALONG, AGAINST, PEER)]


def gather_second(along, peer):
    return [lax.ppermute(along, "seq", ALONG), lax.ppermute(peer, "seq", ALONG), lax.ppermute(peer, "seq", AGAINST)]


def sibling(chunk):
    return lax.ppermute(chunk, "seq", SIBLING)


def body(prompt_query, prompt_key, prompt_value, reply_query, reply_key, reply_value, lengths, out_weight, prompt_grad, reply_grad):
    prompt_rows = prompt_query.shape[0]
    n_seq = lax.axis_size("seq")
    seq, head = lax.axis_index("seq"), lax.axis_index("head")
    scalar = lambda value: value.reshape(1).astype(jnp.int32)
    x, z, core = seq // 8, (seq // 2) % 4, seq % 2
    order = jnp.stack([(z - (1 - 2 * core) * hop) % 4 for hop in (0, 1, -1, 2)]).astype(jnp.int32)
    core, near, other, head = scalar(core), scalar(x), scalar(1 - x), scalar(head)
    own = jnp.concatenate([prompt_key, prompt_value], 1)
    kv = lax.all_to_all(jnp.broadcast_to(own[None], (n_seq,) + own.shape), "seq", 0, 0).reshape(n_seq * prompt_rows, 2 * DIM)
    mine, along, against, peer = gather_first(out_weight.T)
    mine_twin = sibling(mine)
    along, against, peer, mine_twin, kv = lax.optimization_barrier((along, against, peer, mine_twin, kv))
    far, peer_along, peer_against = gather_second(along, peer)
    weights, prompt_weights, reply_att, prompt_att = attention_forward(scalar(seq), lengths, reply_query, prompt_query, kv, reply_key, reply_value)
    along, against, peer, peer_along, reply_att = lax.optimization_barrier((along, against, peer, peer_along, reply_att))
    peer_far = lax.ppermute(peer_along, "seq", ALONG)
    near_chunks = [mine, along, against, far, mine_twin] + [sibling(chunk) for chunk in (along, against, far)]
    far_chunks = [peer, peer_along, peer_against, peer_far]
    far_chunks = far_chunks + [sibling(chunk) for chunk in far_chunks]
    (partial,) = upstream(order, core, near, lengths, near_chunks, prompt_grad, reply_grad, None)
    products = head_products(order, core, head, near, near_chunks, prompt_att, reply_att, ())
    partial, products, far_chunks = lax.optimization_barrier((partial, products, far_chunks))
    kept, sent, *turns = head_products(order, core, head, other, far_chunks, prompt_att, reply_att, products)
    came = lax.ppermute(sent, "head", head_perm(0, 1))
    turned = [lax.ppermute(turns[dy], "head", head_perm(dy, 0)) for dy in (1, 2, 3)]
    prompt_up, reply_up = upstream(order, core, other, lengths, far_chunks, prompt_grad, reply_grad, partial)
    query_grad, prompt_query_grad, kv_grad, reply_key_grad, reply_value_grad = attention_backward(
        weights, prompt_weights, reply_query, reply_up, reply_att, prompt_query, prompt_up, prompt_att, kv, reply_key, reply_value
    )
    first = [(kept[dy].astype(F32) + came[dy].astype(F32)).astype(BF) for dy in range(4)]
    second = turns[0].astype(F32) + turned[0].astype(F32) + turned[1].astype(F32) + turned[2].astype(F32)
    second = second.astype(BF)
    first, second, kv_grad = lax.optimization_barrier((first, (second[0], second[1]), kv_grad))
    first = [first[0]] + [lax.ppermute(first[dy], "head", head_perm(dy, 0)) for dy in (1, 2, 3)]
    second = second[0].astype(F32) + lax.ppermute(second[1], "head", head_perm(0, 1)).astype(F32)
    first = first[0].astype(F32) + first[1].astype(F32) + first[2].astype(F32) + first[3].astype(F32)
    first, second = first.astype(BF), second.astype(BF)
    terms = lax.all_to_all(kv_grad.reshape(n_seq, prompt_rows, 2 * DIM), "seq", 0, 0)
    kv_total = jnp.sum(terms.astype(F32), axis=0).astype(BF)
    return (
        first[:prompt_rows],
        jnp.concatenate([first[prompt_rows:], second], 0),
        prompt_query_grad,
        kv_total[:, :DIM],
        kv_total[:, DIM:],
        query_grad,
        reply_key_grad,
        reply_value_grad,
    )


def solution(mesh):
    cut = P("seq", "head")
    in_specs = (cut, cut, cut, cut, cut, cut, P("seq"), P("head", "seq"), P("seq", None), P("seq", None))
    return jax.shard_map(body, mesh=mesh, in_specs=in_specs, out_specs=(cut,) * 8, check_vma=False)
```

```python
import jax
import jax.numpy as jnp
from jax import lax
from jax.experimental import pallas as pl
from jax.experimental.pallas import tpu as pltpu
from jax.sharding import PartitionSpec as P

DIM = 128
BF = jnp.bfloat16
F32 = jnp.float32
SCALE = DIM**-0.5
EXP_SCALE = SCALE * 1.4426950408889634
PER = 2
VMEM_LIMIT = 60 * 1024 * 1024


def dot_nn(a, b):
    return lax.dot_general(a, b, (((1,), (0,)), ((), ())), preferred_element_type=F32)


def dot_nt(a, b):
    return lax.dot_general(a, b, (((1,), (1,)), ((), ())), preferred_element_type=F32)


def fold(part):
    while part.shape[0] > 8:
        half = part.shape[0] // 2
        part = jnp.maximum(part[:half], part[half:])
    return part


def forward_kernel(
    index_ref, length_ref, query_ref, prompt_query_ref, key_ref, value_ref, reply_key_ref, reply_value_ref,
    weight_ref, prompt_weight_ref, out_ref, prompt_out_ref, inverse_ref, prompt_inverse_ref, value_t, scores, stack,
):
    step = pl.program_id(0)
    heads = pl.num_programs(0) - 1
    prompt = key_ref.shape[0]
    rows = query_ref.shape[0]
    keys = prompt + rows
    prompt_rows = prompt_query_ref.shape[0]

    @pl.when(step == 0)
    def _():
        value_t[:DIM, :prompt] = value_ref[...].T
        value_t[:DIM, prompt:] = reply_value_ref[...].T
        value_t[DIM:, :] = jnp.ones((value_t.shape[0] - DIM, keys), BF)

    def raise_block(slot, block, lanes, shift, seen=None):
        part = scores[slot, block, lanes]
        if seen is not None:
            part = jnp.where(seen, part, -jnp.inf)
        return jnp.exp2(part * EXP_SCALE - shift).astype(BF)

    def divide(total):
        inverse = 1.0 / total[DIM : DIM + 1, :]
        return (total[:DIM, :] * inverse).T, jnp.broadcast_to(inverse, (DIM, rows)).T

    def score(slot):
        query = query_ref[:, slot * DIM : (slot + 1) * DIM]
        half = rows // 2
        upper = None
        for start in range(0, prompt, 256):
            part = dot_nt(key_ref[start : start + 256, :], query)
            scores[slot, start : start + 256, :] = part
            upper = fold(part) if upper is None else jnp.maximum(upper, fold(part))
        scores[slot, prompt : prompt + half, :] = dot_nt(reply_key_ref[:half], query)
        scores[slot, prompt + half :, half:] = dot_nt(reply_key_ref[half:], query[half:])
        return upper

    def weigh(slot, upper):
        seen = lax.broadcasted_iota(jnp.int32, (DIM, DIM), 0) <= lax.broadcasted_iota(jnp.int32, (DIM, DIM), 1)
        for tile in range(rows // DIM):
            lanes = slice(tile * DIM, (tile + 1) * DIM)
            full = prompt + tile * DIM
            top = jnp.maximum(upper[:, lanes], fold(jnp.where(seen, scores[slot, full : full + DIM, lanes], -jnp.inf)))
            for start in range(prompt, full, DIM):
                top = jnp.maximum(top, fold(scores[slot, start : start + DIM, lanes]))
            shift = jnp.max(top, axis=0, keepdims=True) * EXP_SCALE
            for start in range(0, full, DIM):
                block = slice(start, start + DIM)
                weight_ref[slot, block, lanes] = raise_block(slot, block, lanes, shift)
            block = slice(full, full + DIM)
            weight_ref[slot, block, lanes] = raise_block(slot, block, lanes, shift, seen)
            if full + DIM < keys:
                weight_ref[slot, full + DIM :, lanes] = jnp.zeros((keys - full - DIM, DIM), BF)

    def attend(slot):
        lanes = slice(slot * DIM, (slot + 1) * DIM)
        out, inverse = divide(dot_nn(value_t[...], weight_ref[slot]))
        live = lax.broadcasted_iota(jnp.int32, (rows, DIM), 0) < length_ref[0]
        out_ref[:, lanes] = jnp.where(live, out, 0.0).astype(BF)
        inverse_ref[:, lanes] = inverse

    @pl.when(step < heads)
    def _():
        upper = score(0)
        for slot in range(PER):
            following = score(slot + 1) if slot + 1 < PER else None
            weigh(slot, upper)
            attend(slot)
            upper = following

    @pl.when(step == heads)
    def _():
        for head in range(rows // prompt_rows):
            stack[head * prompt_rows : (head + 1) * prompt_rows, :] = prompt_query_ref[:, head * DIM : (head + 1) * DIM]
        scores[0, :prompt, :] = dot_nt(key_ref[...], stack[...])
        place = lax.broadcasted_iota(jnp.int32, (DIM, DIM), 1) % prompt_rows + index_ref[0] * prompt_rows
        for tile in range(rows // DIM):
            lanes = slice(tile * DIM, (tile + 1) * DIM)
            masks = [lax.broadcasted_iota(jnp.int32, (DIM, DIM), 0) + start <= place for start in range(0, prompt, DIM)]
            top = None
            for start, seen in zip(range(0, prompt, DIM), masks):
                part = fold(jnp.where(seen, scores[0, start : start + DIM, lanes], -jnp.inf))
                top = part if top is None else jnp.maximum(top, part)
            top = jnp.max(top, axis=0, keepdims=True)
            for start, seen in zip(range(0, prompt, DIM), masks):
                block = slice(start, start + DIM)
                prompt_weight_ref[block, lanes] = raise_block(0, block, lanes, top * EXP_SCALE, seen)
        out, inverse = divide(dot_nn(value_t[:, :prompt], prompt_weight_ref[...]))
        prompt_inverse_ref[...] = inverse
        out = out.astype(BF)
        for head in range(rows // prompt_rows):
            prompt_out_ref[:, head * DIM : (head + 1) * DIM] = out[head * prompt_rows : (head + 1) * prompt_rows, :]


def attention_forward(index, length, reply_query, prompt_query, kv, reply_key, reply_value):
    rows, columns = reply_query.shape
    prompt_rows = prompt_query.shape[0]
    heads = columns // DIM
    prompt = kv.shape[0]
    keys = prompt + rows
    steps = heads // PER
    last = steps - 1
    whole = lambda shape: pl.BlockSpec(shape, lambda g: (0, 0))
    return pl.pallas_call(
        forward_kernel,
        grid=(steps + 1,),
        in_specs=[
            pl.BlockSpec(memory_space=pltpu.SMEM),
            pl.BlockSpec(memory_space=pltpu.SMEM),
            pl.BlockSpec((rows, PER * DIM), lambda g: (0, jnp.minimum(g, last))),
            whole((prompt_rows, columns)),
            pl.BlockSpec((prompt, DIM), lambda g: (0, 0)),
            pl.BlockSpec((prompt, DIM), lambda g: (0, 1)),
            whole((rows, DIM)),
            whole((rows, DIM)),
        ],
        out_specs=[
            pl.BlockSpec((PER, keys, rows), lambda g: (jnp.minimum(g, last), 0, 0)),
            whole((prompt, rows)),
            pl.BlockSpec((rows, PER * DIM), lambda g: (0, jnp.minimum(g, last))),
            whole((prompt_rows, columns)),
            pl.BlockSpec((rows, PER * DIM), lambda g: (0, jnp.minimum(g, last))),
            whole((rows, DIM)),
        ],
        out_shape=[
            jax.ShapeDtypeStruct((heads, keys, rows), BF),
            jax.ShapeDtypeStruct((prompt, rows), BF),
            jax.ShapeDtypeStruct((rows, columns), BF),
            jax.ShapeDtypeStruct((prompt_rows, columns), BF),
            jax.ShapeDtypeStruct((rows, columns), F32),
            jax.ShapeDtypeStruct((rows, DIM), F32),
        ],
        scratch_shapes=[
            pltpu.VMEM((DIM + 16, keys), BF),
            pltpu.VMEM((PER, keys, rows), F32),
            pltpu.VMEM((rows, DIM), BF),
        ],
        compiler_params=pltpu.CompilerParams(vmem_limit_bytes=VMEM_LIMIT),
        cost_estimate=pl.CostEstimate(flops=4 * heads * keys * rows * DIM, bytes_accessed=18 * 2**20, transcendentals=heads * keys * rows),
        name="attention_forward",
    )(index, length, reply_query, prompt_query, kv, kv, reply_key, reply_value)


def backward_kernel(
    weight_ref, prompt_weight_ref, query_ref, grad_ref, out_ref, prompt_query_ref, prompt_grad_ref, prompt_out_ref,
    inverse_ref, prompt_inverse_ref, key_ref, value_ref, reply_key_ref, reply_value_ref,
    query_grad_ref, prompt_query_grad_ref, kv_grad_ref, reply_key_grad_ref, reply_value_grad_ref,
    key_t, score_grad, key_grad, value_grad, stack,
):
    step = pl.program_id(0)
    heads = pl.num_programs(0) - 1
    prompt = key_ref.shape[0]
    rows = query_ref.shape[0]
    keys = prompt + rows
    half = rows // 2
    prompt_rows = prompt_query_ref.shape[0]

    @pl.when(step == 0)
    def _():
        key_t[:, :prompt] = key_ref[...].T
        key_t[:, prompt:] = reply_key_ref[...].T
        key_grad[...] = jnp.zeros_like(key_grad)
        value_grad[...] = jnp.zeros_like(value_grad)
        score_grad[:, prompt + half :, :half] = jnp.zeros((PER, half, half), BF)

    def row_delta(grad, out):
        return jnp.sum((grad.astype(F32) * out.astype(F32)).T, axis=0, keepdims=True)

    def key_block(slot, weight, value, grad, query, delta, start, size, low):
        block = slice(start, start + size)
        slope = dot_nt(value, grad)
        part = (weight.astype(F32) * (slope - delta)).astype(BF)
        score_grad[slot, block, low:] = part
        key_grad[block, :] += dot_nn(part, query)
        value_grad[block, :] += dot_nn(weight, grad)

    @pl.when(step < heads)
    def _():
        for slot in range(PER):
            lanes = slice(slot * DIM, (slot + 1) * DIM)
            query, grad = query_ref[:, lanes], (grad_ref[:, lanes].astype(F32) * inverse_ref[:, lanes]).astype(BF)
            delta = row_delta(grad, out_ref[:, lanes])
            for start in range(0, prompt, 512):
                key_block(slot, weight_ref[slot, start : start + 512, :], value_ref[start : start + 512, :], grad, query, delta, start, 512, 0)
            key_block(slot, weight_ref[slot, prompt : prompt + half, :], reply_value_ref[:half], grad, query, delta, prompt, half, 0)
            key_block(
                slot, weight_ref[slot, prompt + half :, half:], reply_value_ref[half:], grad[half:], query[half:], delta[:, half:],
                prompt + half, half, half,
            )
            query_grad_ref[:, lanes] = (dot_nn(key_t[...], score_grad[slot]).T * SCALE).astype(BF)

    @pl.when(step == heads)
    def _():
        count = rows // prompt_rows
        for head in range(count):
            place, lanes = slice(head * prompt_rows, (head + 1) * prompt_rows), slice(head * DIM, (head + 1) * DIM)
            stack[0, place, :] = prompt_query_ref[:, lanes]
            stack[1, place, :] = prompt_grad_ref[:, lanes]
            stack[2, place, :] = prompt_out_ref[:, lanes]
        query, grad = stack[0], (stack[1].astype(F32) * prompt_inverse_ref[...]).astype(BF)
        delta = row_delta(grad, stack[2])
        for start in range(0, prompt, 512):
            key_block(0, prompt_weight_ref[start : start + 512, :], value_ref[start : start + 512, :], grad, query, delta, start, 512, 0)
        result = (dot_nn(key_t[:, :prompt], score_grad[0, :prompt, :]).T * SCALE).astype(BF)
        for head in range(count):
            prompt_query_grad_ref[:, head * DIM : (head + 1) * DIM] = result[head * prompt_rows : (head + 1) * prompt_rows, :]
        kv_grad_ref[:, :DIM] = (key_grad[:prompt, :] * SCALE).astype(BF)
        kv_grad_ref[:, DIM:] = value_grad[:prompt, :].astype(BF)
        reply_key_grad_ref[...] = (key_grad[prompt:, :] * SCALE).astype(BF)
        reply_value_grad_ref[...] = value_grad[prompt:, :].astype(BF)


def attention_backward(weights, prompt_weights, inverse, prompt_inverse, reply_query, reply_up, reply_att, prompt_query, prompt_up, prompt_att, kv, reply_key, reply_value):
    rows, columns = reply_query.shape
    prompt_rows = prompt_query.shape[0]
    heads = columns // DIM
    prompt = kv.shape[0]
    keys = prompt + rows
    steps = heads // PER
    last = steps - 1
    whole = lambda shape: pl.BlockSpec(shape, lambda g: (0, 0))
    column = pl.BlockSpec((rows, PER * DIM), lambda g: (0, jnp.minimum(g, last)))
    return pl.pallas_call(
        backward_kernel,
        grid=(steps + 1,),
        in_specs=[
            pl.BlockSpec((PER, keys, rows), lambda g: (jnp.minimum(g, last), 0, 0)),
            whole((prompt, rows)),
            column,
            column,
            column,
            whole((prompt_rows, columns)),
            whole((prompt_rows, columns)),
            whole((prompt_rows, columns)),
            column,
            whole((rows, DIM)),
            pl.BlockSpec((prompt, DIM), lambda g: (0, 0)),
            pl.BlockSpec((prompt, DIM), lambda g: (0, 1)),
            whole((rows, DIM)),
            whole((rows, DIM)),
        ],
        out_specs=[
            column,
            whole((prompt_rows, columns)),
            whole((prompt, 2 * DIM)),
            whole((rows, DIM)),
            whole((rows, DIM)),
        ],
        out_shape=[
            jax.ShapeDtypeStruct((rows, columns), BF),
            jax.ShapeDtypeStruct((prompt_rows, columns), BF),
            jax.ShapeDtypeStruct((prompt, 2 * DIM), BF),
            jax.ShapeDtypeStruct((rows, DIM), BF),
            jax.ShapeDtypeStruct((rows, DIM), BF),
        ],
        scratch_shapes=[
            pltpu.VMEM((DIM, keys), BF),
            pltpu.VMEM((PER, keys, rows), BF),
            pltpu.VMEM((keys, DIM), F32),
            pltpu.VMEM((keys, DIM), F32),
            pltpu.VMEM((3, rows, DIM), BF),
        ],
        compiler_params=pltpu.CompilerParams(vmem_limit_bytes=VMEM_LIMIT),
        cost_estimate=pl.CostEstimate(flops=8 * heads * keys * rows * DIM, bytes_accessed=18 * 2**20, transcendentals=0),
        name="attention_backward",
    )(weights, prompt_weights, reply_query, reply_up, reply_att, prompt_query, prompt_up, prompt_att, inverse, prompt_inverse, kv, kv, reply_key, reply_value)


def half_copies(chunks, order_ref, core_ref, gathered, sems):
    size = chunks[0].shape[0]
    core = core_ref[0]
    copies = []
    for slot in range(4):
        for side in range(2):
            place = order_ref[slot if side == 0 else SWAPPED[slot]]
            row = place * (2 * size) + (core if side == 0 else 1 - core) * size
            copies.append(
                pltpu.make_async_copy(
                    chunks[side * 4 + slot],
                    gathered.at[pl.ds(pl.multiple_of(row, size), size), :],
                    sems.at[place, side],
                )
            )
    return copies


def products_kernel(order_ref, core_ref, head_ref, half_ref, *refs):
    chunks = refs[:8]
    prompt_ref, reply_ref = refs[8:10]
    outs, (gathered, rows, held, sems, out_sems) = refs[-11:-5], refs[-5:]
    size = chunks[0].shape[0]
    for copy in half_copies(chunks, order_ref, core_ref, gathered, sems):
        copy.start()
    count = prompt_ref.shape[0]
    half = rows.shape[0] // 2
    rows[:count, :] = prompt_ref[...]
    rows[count:, :] = reply_ref[...]
    across, along = head_ref[0] % 2, head_ref[0] // 2

    def flush(slot, dy, dx):
        upper = [
            pltpu.make_async_copy(held.at[slot, pl.ds(0, half), :], outs[side].at[dy], out_sems.at[slot, 0]) for side in range(2)
        ]
        lower = [
            pltpu.make_async_copy(held.at[slot, pl.ds(half, half), :], outs[2 + turn].at[dx], out_sems.at[slot, 1]) for turn in range(4)
        ]
        return upper, lower

    for place in range(4):
        slot = place % 2
        if place >= 2:
            upper, lower = flush(slot, 0, 0)
            upper[0].wait()
            lower[0].wait()
        for side in range(2):
            pltpu.make_async_copy(chunks[side * 4], gathered.at[pl.ds(0, size), :], sems.at[place, side]).wait()
        block = gathered[2 * size * place : 2 * size * (place + 1), :]
        held[slot] = dot_nt(rows[...], block).astype(BF)
        target = half_ref[0] * 4 + place
        dy, dx = (target // 2 - along + 4) % 4, (target % 2 - across + 2) % 2
        upper, lower = flush(slot, dy, dx)
        for side in range(2):
            pl.when(dx == side)(upper[side].start)
        for turn in range(4):
            pl.when(dy == turn)(lower[turn].start)
    for slot in range(2):
        upper, lower = flush(slot, 0, 0)
        upper[0].wait()
        lower[0].wait()


def head_products(order, core, head, half, chunks, prompt_att, reply_att, earlier):
    total = prompt_att.shape[0] + reply_att.shape[0]
    size, depth = chunks[0].shape
    width = 2 * size
    anywhere = pl.BlockSpec(memory_space=pl.ANY)
    scalar = pl.BlockSpec(memory_space=pltpu.SMEM)
    return pl.pallas_call(
        products_kernel,
        in_specs=[scalar] * 4 + [anywhere] * 8 + [pl.BlockSpec(memory_space=pltpu.VMEM)] * 2 + [anywhere] * len(earlier),
        out_specs=[anywhere] * 6,
        out_shape=[jax.ShapeDtypeStruct((4, total // 2, width), BF)] * 2 + [jax.ShapeDtypeStruct((2, total // 2, width), BF)] * 4,
        input_output_aliases={14 + place: place for place in range(len(earlier))},
        scratch_shapes=[
            pltpu.VMEM((8 * size, depth), BF),
            pltpu.VMEM((total, depth), BF),
            pltpu.VMEM((2, total, width), BF),
            pltpu.SemaphoreType.DMA((4, 2)),
            pltpu.SemaphoreType.DMA((2, 2)),
        ],
        compiler_params=pltpu.CompilerParams(vmem_limit_bytes=VMEM_LIMIT),
        cost_estimate=pl.CostEstimate(flops=2 * total * depth * 8 * size, bytes_accessed=9 * 2**20, transcendentals=0),
        name="head_products",
    )(order, core, head, half, *chunks, prompt_att, reply_att, *earlier)


def upstream_kernel(order_ref, core_ref, half_ref, length_ref, *refs):
    chunks = refs[:8]
    prompt_ref, reply_ref = refs[8:10]
    last = len(refs) == 17
    earlier, outs, (gathered, rows, sems, row_sems) = (refs[10:11], refs[11:13], refs[13:]) if last else ((), refs[10:11], refs[11:])
    step = pl.program_id(0)
    count = prompt_ref.shape[0]

    @pl.when(step == 0)
    def _():
        columns = pl.ds(pl.multiple_of(half_ref[0] * rows.shape[1], rows.shape[1]), rows.shape[1])
        copies = half_copies(chunks, order_ref, core_ref, gathered, sems)
        copies.append(pltpu.make_async_copy(prompt_ref.at[:, columns], rows.at[pl.ds(0, count), :], row_sems.at[0]))
        copies.append(pltpu.make_async_copy(reply_ref.at[:, columns], rows.at[pl.ds(count, rows.shape[0] - count), :], row_sems.at[1]))
        for copy in copies:
            copy.start()
        for copy in copies:
            copy.wait()

    width = outs[0].shape[1]
    total = dot_nn(rows[...], gathered[:, pl.ds(pl.multiple_of(step * width, width), width)])
    if not last:
        outs[0][...] = total
    else:
        total = total + earlier[0][...]
        outs[0][...] = total[:count].astype(BF)
        live = lax.broadcasted_iota(jnp.int32, (total.shape[0] - count, width), 0) < length_ref[0]
        outs[1][...] = jnp.where(live, total[count:], 0.0).astype(BF)


def upstream(order, core, half, lengths, chunks, prompt_grad, reply_grad, earlier):
    size, depth = chunks[0].shape
    prompt_rows, reply_rows = prompt_grad.shape[0], reply_grad.shape[0]
    total = prompt_rows + reply_rows
    parts = 2
    anywhere = pl.BlockSpec(memory_space=pl.ANY)
    scalar = pl.BlockSpec(memory_space=pltpu.SMEM)
    column = lambda rows: pl.BlockSpec((rows, depth // parts), lambda k: (0, k))
    if earlier is None:
        out_specs, out_shape = [column(total)], [jax.ShapeDtypeStruct((total, depth), F32)]
    else:
        out_specs = [column(prompt_rows), column(reply_rows)]
        out_shape = [jax.ShapeDtypeStruct((prompt_rows, depth), BF), jax.ShapeDtypeStruct((reply_rows, depth), BF)]
    return pl.pallas_call(
        upstream_kernel,
        grid=(parts,),
        in_specs=[scalar] * 4 + [anywhere] * 10 + ([] if earlier is None else [column(total)]),
        out_specs=out_specs,
        out_shape=out_shape,
        scratch_shapes=[
            pltpu.VMEM((8 * size, depth), BF),
            pltpu.VMEM((total, 8 * size), BF),
            pltpu.SemaphoreType.DMA((4, 2)),
            pltpu.SemaphoreType.DMA((2,)),
        ],
        compiler_params=pltpu.CompilerParams(vmem_limit_bytes=VMEM_LIMIT),
        cost_estimate=pl.CostEstimate(flops=2 * total * depth * 8 * size, bytes_accessed=9 * 2**20, transcendentals=0),
        name="upstream",
    )(order, core, half, lengths, *chunks, prompt_grad, reply_grad, *([] if earlier is None else [earlier]))


SWAPPED = (0, 2, 1, 3)


def seq_perm(move):
    pairs = []
    for x in range(2):
        for z in range(4):
            for core in range(2):
                to_x, to_z, to_core = move(x, z, core)
                pairs.append((x * 8 + z * 2 + core, (to_x % 2) * 8 + (to_z % 4) * 2 + to_core % 2))
    return pairs


ALONG = seq_perm(lambda x, z, core: (x, z + 1 - 2 * core, core))
AGAINST = seq_perm(lambda x, z, core: (x, z - 1 + 2 * core, core))
PEER = seq_perm(lambda x, z, core: (x + 1, z, core))
SIBLING = seq_perm(lambda x, z, core: (x, z, core + 1))


def head_perm(dy, dx):
    return [(y * 2 + x, ((y + dy) % 4) * 2 + (x + dx) % 2) for y in range(4) for x in range(2)]


def body(prompt_query, prompt_key, prompt_value, reply_query, reply_key, reply_value, lengths, out_weight, prompt_grad, reply_grad):
    prompt_rows = prompt_query.shape[0]
    n_seq = lax.axis_size("seq")
    seq, head = lax.axis_index("seq"), lax.axis_index("head")
    scalar = lambda value: value.reshape(1).astype(jnp.int32)
    x, z, core = seq // 8, (seq // 2) % 4, seq % 2
    order = jnp.stack([(z - (1 - 2 * core) * hop) % 4 for hop in (0, 1, -1, 2)]).astype(jnp.int32)
    core, near, other, head = scalar(core), scalar(x), scalar(1 - x), scalar(head)
    own = jnp.concatenate([prompt_key, prompt_value], 1)
    kv = lax.all_to_all(jnp.broadcast_to(own[None], (n_seq,) + own.shape), "seq", 0, 0).reshape(n_seq * prompt_rows, 2 * DIM)
    mine = out_weight.T
    send = lambda chunk, perm: lax.ppermute(chunk, "seq", perm)
    along, against, peer = [send(mine, perm) for perm in (ALONG, AGAINST, PEER)]
    along, against, peer, kv = lax.optimization_barrier((along, against, peer, kv))
    far, peer_along = send(along, ALONG), send(peer, ALONG)
    near_twins = [send(chunk, SIBLING) for chunk in (mine, along, against)]
    weights, prompt_weights, reply_att, prompt_att, inverse, prompt_inverse = attention_forward(
        scalar(seq), lengths, reply_query, prompt_query, kv, reply_key, reply_value
    )
    far, peer, peer_along, near_twins, reply_att = lax.optimization_barrier((far, peer, peer_along, near_twins, reply_att))
    near_chunks = [mine, along, against, far, *near_twins, send(far, SIBLING)]
    peer_against, peer_far = send(peer, AGAINST), send(peer_along, ALONG)
    peer_twins = [send(chunk, SIBLING) for chunk in (peer, peer_along)]
    (partial,) = upstream(order, core, near, lengths, near_chunks, prompt_grad, reply_grad, None)
    products = head_products(order, core, head, near, near_chunks, prompt_att, reply_att, ())
    partial, products, peer_against, peer_far = lax.optimization_barrier((partial, products, peer_against, peer_far))
    peer_twins = peer_twins + [send(chunk, SIBLING) for chunk in (peer_against, peer_far)]
    far_chunks = [peer, peer_along, peer_against, peer_far, *peer_twins]
    kept, sent, *turns = head_products(order, core, head, other, far_chunks, prompt_att, reply_att, products)
    came = lax.ppermute(sent, "head", head_perm(0, 1))
    turned = [lax.ppermute(turns[dy], "head", head_perm(dy, 0)) for dy in (1, 2, 3)]
    prompt_up, reply_up = upstream(order, core, other, lengths, far_chunks, prompt_grad, reply_grad, partial)
    query_grad, prompt_query_grad, kv_grad, reply_key_grad, reply_value_grad = attention_backward(
        weights, prompt_weights, inverse, prompt_inverse, reply_query, reply_up, reply_att, prompt_query, prompt_up, prompt_att, kv, reply_key, reply_value
    )
    first = [(kept[dy].astype(F32) + came[dy].astype(F32)).astype(BF) for dy in range(4)]
    second = turns[0].astype(F32) + turned[0].astype(F32) + turned[1].astype(F32) + turned[2].astype(F32)
    second = second.astype(BF)
    first, second, kv_grad = lax.optimization_barrier((first, (second[0], second[1]), kv_grad))
    first = [first[0]] + [lax.ppermute(first[dy], "head", head_perm(dy, 0)) for dy in (1, 2, 3)]
    second = second[0].astype(F32) + lax.ppermute(second[1], "head", head_perm(0, 1)).astype(F32)
    first = first[0].astype(F32) + first[1].astype(F32) + first[2].astype(F32) + first[3].astype(F32)
    first, second = first.astype(BF), second.astype(BF)
    terms = lax.all_to_all(kv_grad.reshape(n_seq, prompt_rows, 2 * DIM), "seq", 0, 0)
    kv_total = jnp.sum(terms.astype(F32), axis=0).astype(BF)
    return (
        first[:prompt_rows],
        jnp.concatenate([first[prompt_rows:], second], 0),
        prompt_query_grad,
        kv_total[:, :DIM],
        kv_total[:, DIM:],
        query_grad,
        reply_key_grad,
        reply_value_grad,
    )


def solution(mesh):
    cut = P("seq", "head")
    in_specs = (cut, cut, cut, cut, cut, cut, P("seq"), P("head", "seq"), P("seq", None), P("seq", None))
    return jax.shard_map(body, mesh=mesh, in_specs=in_specs, out_specs=(cut,) * 8, check_vma=False)
```

```python
import functools

import jax
import jax.numpy as jnp
from jax import lax
from jax.experimental import pallas as pl
from jax.experimental.pallas import tpu as pltpu
from jax.sharding import PartitionSpec as P

DIM = 128
BF = jnp.bfloat16
F32 = jnp.float32
SCALE = DIM**-0.5
EXP_SCALE = SCALE * 1.4426950408889634
PER = 2
VMEM_LIMIT = 60 * 1024 * 1024


def dot_nn(a, b):
    return lax.dot_general(a, b, (((1,), (0,)), ((), ())), preferred_element_type=F32)


def dot_nt(a, b):
    return lax.dot_general(a, b, (((1,), (1,)), ((), ())), preferred_element_type=F32)


def fold(part):
    while part.shape[0] > 8:
        half = part.shape[0] // 2
        part = jnp.maximum(part[:half], part[half:])
    return part


def forward_kernel(
    index_ref, length_ref, query_ref, prompt_query_ref, key_ref, value_ref, reply_key_ref, reply_value_ref,
    weight_ref, prompt_weight_ref, out_ref, prompt_out_ref, inverse_ref, prompt_inverse_ref, value_t, scores, stack,
):
    step = pl.program_id(0)
    heads = pl.num_programs(0) - 1
    prompt = key_ref.shape[0]
    rows = query_ref.shape[0]
    keys = prompt + rows
    prompt_rows = prompt_query_ref.shape[0]

    @pl.when(step == 0)
    def _():
        value_t[:DIM, :prompt] = value_ref[...].T
        value_t[:DIM, prompt:] = reply_value_ref[...].T
        value_t[DIM:, :] = jnp.ones((value_t.shape[0] - DIM, keys), BF)

    def raise_block(slot, block, lanes, shift, seen=None):
        part = scores[slot, block, lanes]
        if seen is not None:
            part = jnp.where(seen, part, -jnp.inf)
        return jnp.exp2(part * EXP_SCALE - shift).astype(BF)

    def divide(total):
        inverse = 1.0 / total[DIM : DIM + 1, :]
        return (total[:DIM, :] * inverse).T, jnp.broadcast_to(inverse, (DIM, rows)).T

    def score(slot):
        query = query_ref[:, slot * DIM : (slot + 1) * DIM]
        half = rows // 2
        upper = None
        for start in range(0, prompt, 256):
            part = dot_nt(key_ref[start : start + 256, :], query)
            scores[slot, start : start + 256, :] = part
            upper = fold(part) if upper is None else jnp.maximum(upper, fold(part))
        scores[slot, prompt : prompt + half, :] = dot_nt(reply_key_ref[:half], query)
        scores[slot, prompt + half :, half:] = dot_nt(reply_key_ref[half:], query[half:])
        return upper

    def weigh(slot, upper):
        seen = lax.broadcasted_iota(jnp.int32, (DIM, DIM), 0) <= lax.broadcasted_iota(jnp.int32, (DIM, DIM), 1)
        for tile in range(rows // DIM):
            lanes = slice(tile * DIM, (tile + 1) * DIM)
            full = prompt + tile * DIM
            top = jnp.maximum(upper[:, lanes], fold(jnp.where(seen, scores[slot, full : full + DIM, lanes], -jnp.inf)))
            for start in range(prompt, full, DIM):
                top = jnp.maximum(top, fold(scores[slot, start : start + DIM, lanes]))
            shift = jnp.max(top, axis=0, keepdims=True) * EXP_SCALE
            for start in range(0, full, DIM):
                block = slice(start, start + DIM)
                weight_ref[slot, block, lanes] = raise_block(slot, block, lanes, shift)
            block = slice(full, full + DIM)
            weight_ref[slot, block, lanes] = raise_block(slot, block, lanes, shift, seen)
            if full + DIM < keys:
                weight_ref[slot, full + DIM :, lanes] = jnp.zeros((keys - full - DIM, DIM), BF)

    def attend(slot):
        lanes = slice(slot * DIM, (slot + 1) * DIM)
        out, inverse = divide(dot_nn(value_t[...], weight_ref[slot]))
        live = lax.broadcasted_iota(jnp.int32, (rows, DIM), 0) < length_ref[0]
        out_ref[:, lanes] = jnp.where(live, out, 0.0).astype(BF)
        inverse_ref[:, lanes] = inverse

    @pl.when(step < heads)
    def _():
        upper = score(0)
        for slot in range(PER):
            following = score(slot + 1) if slot + 1 < PER else None
            weigh(slot, upper)
            attend(slot)
            upper = following

    @pl.when(step == heads)
    def _():
        for head in range(rows // prompt_rows):
            stack[head * prompt_rows : (head + 1) * prompt_rows, :] = prompt_query_ref[:, head * DIM : (head + 1) * DIM]
        scores[0, :prompt, :] = dot_nt(key_ref[...], stack[...])
        place = lax.broadcasted_iota(jnp.int32, (DIM, DIM), 1) % prompt_rows + index_ref[0] * prompt_rows
        for tile in range(rows // DIM):
            lanes = slice(tile * DIM, (tile + 1) * DIM)
            masks = [lax.broadcasted_iota(jnp.int32, (DIM, DIM), 0) + start <= place for start in range(0, prompt, DIM)]
            top = None
            for start, seen in zip(range(0, prompt, DIM), masks):
                part = fold(jnp.where(seen, scores[0, start : start + DIM, lanes], -jnp.inf))
                top = part if top is None else jnp.maximum(top, part)
            top = jnp.max(top, axis=0, keepdims=True)
            for start, seen in zip(range(0, prompt, DIM), masks):
                block = slice(start, start + DIM)
                prompt_weight_ref[block, lanes] = raise_block(0, block, lanes, top * EXP_SCALE, seen)
        out, inverse = divide(dot_nn(value_t[:, :prompt], prompt_weight_ref[...]))
        prompt_inverse_ref[...] = inverse
        out = out.astype(BF)
        for head in range(rows // prompt_rows):
            prompt_out_ref[:, head * DIM : (head + 1) * DIM] = out[head * prompt_rows : (head + 1) * prompt_rows, :]


def attention_forward(index, length, reply_query, prompt_query, kv, reply_key, reply_value):
    rows, columns = reply_query.shape
    prompt_rows = prompt_query.shape[0]
    heads = columns // DIM
    prompt = kv.shape[0]
    keys = prompt + rows
    steps = heads // PER
    last = steps - 1
    whole = lambda shape: pl.BlockSpec(shape, lambda g: (0, 0))
    return pl.pallas_call(
        forward_kernel,
        grid=(steps + 1,),
        in_specs=[
            pl.BlockSpec(memory_space=pltpu.SMEM),
            pl.BlockSpec(memory_space=pltpu.SMEM),
            pl.BlockSpec((rows, PER * DIM), lambda g: (0, jnp.minimum(g, last))),
            whole((prompt_rows, columns)),
            pl.BlockSpec((prompt, DIM), lambda g: (0, 0)),
            pl.BlockSpec((prompt, DIM), lambda g: (0, 1)),
            whole((rows, DIM)),
            whole((rows, DIM)),
        ],
        out_specs=[
            pl.BlockSpec((PER, keys, rows), lambda g: (jnp.minimum(g, last), 0, 0)),
            whole((prompt, rows)),
            pl.BlockSpec((rows, PER * DIM), lambda g: (0, jnp.minimum(g, last))),
            whole((prompt_rows, columns)),
            pl.BlockSpec((rows, PER * DIM), lambda g: (0, jnp.minimum(g, last))),
            whole((rows, DIM)),
        ],
        out_shape=[
            jax.ShapeDtypeStruct((heads, keys, rows), BF),
            jax.ShapeDtypeStruct((prompt, rows), BF),
            jax.ShapeDtypeStruct((rows, columns), BF),
            jax.ShapeDtypeStruct((prompt_rows, columns), BF),
            jax.ShapeDtypeStruct((rows, columns), F32),
            jax.ShapeDtypeStruct((rows, DIM), F32),
        ],
        scratch_shapes=[
            pltpu.VMEM((DIM + 16, keys), BF),
            pltpu.VMEM((PER, keys, rows), F32),
            pltpu.VMEM((rows, DIM), BF),
        ],
        compiler_params=pltpu.CompilerParams(vmem_limit_bytes=VMEM_LIMIT),
        cost_estimate=pl.CostEstimate(flops=4 * heads * keys * rows * DIM, bytes_accessed=18 * 2**20, transcendentals=heads * keys * rows),
        name="attention_forward",
    )(index, length, reply_query, prompt_query, kv, kv, reply_key, reply_value)


def backward_kernel(
    weight_ref, prompt_weight_ref, query_ref, grad_ref, out_ref, prompt_query_ref, prompt_grad_ref, prompt_out_ref,
    inverse_ref, prompt_inverse_ref, key_ref, value_ref, reply_key_ref, reply_value_ref,
    query_grad_ref, prompt_query_grad_ref, kv_grad_ref, reply_key_grad_ref, reply_value_grad_ref,
    key_t, score_grad, key_grad, value_grad, stack,
):
    step = pl.program_id(0)
    heads = pl.num_programs(0) - 1
    prompt = key_ref.shape[0]
    rows = query_ref.shape[0]
    keys = prompt + rows
    half = rows // 2
    prompt_rows = prompt_query_ref.shape[0]

    @pl.when(step == 0)
    def _():
        key_t[:, :prompt] = key_ref[...].T
        key_t[:, prompt:] = reply_key_ref[...].T
        key_grad[...] = jnp.zeros_like(key_grad)
        value_grad[...] = jnp.zeros_like(value_grad)
        score_grad[:, prompt + half :, :half] = jnp.zeros((PER, half, half), BF)

    def row_delta(grad, out):
        return jnp.sum((grad.astype(F32) * out.astype(F32)).T, axis=0, keepdims=True)

    def key_block(slot, weight, value, grad, query, delta, start, size, low):
        block = slice(start, start + size)
        slope = dot_nt(value, grad)
        part = (weight.astype(F32) * (slope - delta)).astype(BF)
        score_grad[slot, block, low:] = part
        key_grad[block, :] += dot_nn(part, query)
        value_grad[block, :] += dot_nn(weight, grad)

    @pl.when(step < heads)
    def _():
        for slot in range(PER):
            lanes = slice(slot * DIM, (slot + 1) * DIM)
            query, grad = query_ref[:, lanes], (grad_ref[:, lanes].astype(F32) * inverse_ref[:, lanes]).astype(BF)
            delta = row_delta(grad, out_ref[:, lanes])
            for start in range(0, prompt, 512):
                key_block(slot, weight_ref[slot, start : start + 512, :], value_ref[start : start + 512, :], grad, query, delta, start, 512, 0)
            key_block(slot, weight_ref[slot, prompt : prompt + half, :], reply_value_ref[:half], grad, query, delta, prompt, half, 0)
            key_block(
                slot, weight_ref[slot, prompt + half :, half:], reply_value_ref[half:], grad[half:], query[half:], delta[:, half:],
                prompt + half, half, half,
            )
            query_grad_ref[:, lanes] = (dot_nn(key_t[...], score_grad[slot]).T * SCALE).astype(BF)

    @pl.when(step == heads)
    def _():
        count = rows // prompt_rows
        for head in range(count):
            place, lanes = slice(head * prompt_rows, (head + 1) * prompt_rows), slice(head * DIM, (head + 1) * DIM)
            stack[0, place, :] = prompt_query_ref[:, lanes]
            stack[1, place, :] = prompt_grad_ref[:, lanes]
            stack[2, place, :] = prompt_out_ref[:, lanes]
        query, grad = stack[0], (stack[1].astype(F32) * prompt_inverse_ref[...]).astype(BF)
        delta = row_delta(grad, stack[2])
        for start in range(0, prompt, 512):
            key_block(0, prompt_weight_ref[start : start + 512, :], value_ref[start : start + 512, :], grad, query, delta, start, 512, 0)
        result = (dot_nn(key_t[:, :prompt], score_grad[0, :prompt, :]).T * SCALE).astype(BF)
        for head in range(count):
            prompt_query_grad_ref[:, head * DIM : (head + 1) * DIM] = result[head * prompt_rows : (head + 1) * prompt_rows, :]
        kv_grad_ref[:, :DIM] = (key_grad[:prompt, :] * SCALE).astype(BF)
        kv_grad_ref[:, DIM:] = value_grad[:prompt, :].astype(BF)
        reply_key_grad_ref[...] = (key_grad[prompt:, :] * SCALE).astype(BF)
        reply_value_grad_ref[...] = value_grad[prompt:, :].astype(BF)


def attention_backward(weights, prompt_weights, inverse, prompt_inverse, reply_query, reply_up, reply_att, prompt_query, prompt_up, prompt_att, kv, reply_key, reply_value):
    rows, columns = reply_query.shape
    prompt_rows = prompt_query.shape[0]
    heads = columns // DIM
    prompt = kv.shape[0]
    keys = prompt + rows
    steps = heads // PER
    last = steps - 1
    whole = lambda shape: pl.BlockSpec(shape, lambda g: (0, 0))
    column = pl.BlockSpec((rows, PER * DIM), lambda g: (0, jnp.minimum(g, last)))
    return pl.pallas_call(
        backward_kernel,
        grid=(steps + 1,),
        in_specs=[
            pl.BlockSpec((PER, keys, rows), lambda g: (jnp.minimum(g, last), 0, 0)),
            whole((prompt, rows)),
            column,
            column,
            column,
            whole((prompt_rows, columns)),
            whole((prompt_rows, columns)),
            whole((prompt_rows, columns)),
            column,
            whole((rows, DIM)),
            pl.BlockSpec((prompt, DIM), lambda g: (0, 0)),
            pl.BlockSpec((prompt, DIM), lambda g: (0, 1)),
            whole((rows, DIM)),
            whole((rows, DIM)),
        ],
        out_specs=[
            column,
            whole((prompt_rows, columns)),
            whole((prompt, 2 * DIM)),
            whole((rows, DIM)),
            whole((rows, DIM)),
        ],
        out_shape=[
            jax.ShapeDtypeStruct((rows, columns), BF),
            jax.ShapeDtypeStruct((prompt_rows, columns), BF),
            jax.ShapeDtypeStruct((prompt, 2 * DIM), BF),
            jax.ShapeDtypeStruct((rows, DIM), BF),
            jax.ShapeDtypeStruct((rows, DIM), BF),
        ],
        scratch_shapes=[
            pltpu.VMEM((DIM, keys), BF),
            pltpu.VMEM((PER, keys, rows), BF),
            pltpu.VMEM((keys, DIM), F32),
            pltpu.VMEM((keys, DIM), F32),
            pltpu.VMEM((3, rows, DIM), BF),
        ],
        compiler_params=pltpu.CompilerParams(vmem_limit_bytes=VMEM_LIMIT),
        cost_estimate=pl.CostEstimate(flops=8 * heads * keys * rows * DIM, bytes_accessed=18 * 2**20, transcendentals=0),
        name="attention_backward",
    )(weights, prompt_weights, reply_query, reply_up, reply_att, prompt_query, prompt_up, prompt_att, inverse, prompt_inverse, kv, kv, reply_key, reply_value)


def absorb_kernel(project, back, resume, order_ref, core_ref, head_ref, half_ref, length_ref, *refs):
    refs = list(refs)
    take = lambda count: [refs.pop(0) for _ in range(count)]
    chunks = take(8)
    sides = []
    if project:
        sides.append(take(2))
    if back:
        sides.append(take(2))
    (earlier,) = take(1) if back and resume else (None,)
    if project and resume:
        take(6)
    outs = take(6) if project else None
    ups = take(2 if resume else 1) if back else None
    gathered, sems = take(2)
    if project:
        rows, held, row_sems, out_sems = take(4)
    if back:
        grads, grad_sems = take(2)
        total, total_sem = take(2) if resume else (ups[0], None)
    size, core = chunks[0].shape[0], core_ref[0]
    width = 2 * size

    copies = []
    if project:
        prompt_ref, reply_ref = sides[0]
        count = prompt_ref.shape[0]
        row_copies = [
            pltpu.make_async_copy(prompt_ref, rows.at[pl.ds(0, count), :], row_sems.at[0]),
            pltpu.make_async_copy(reply_ref, rows.at[pl.ds(count, reply_ref.shape[0]), :], row_sems.at[1]),
        ]
        copies += row_copies
    if back:
        prompt_ref, reply_ref = sides[-1]
        count = prompt_ref.shape[0]
        columns = pl.ds(pl.multiple_of(half_ref[0] * (4 * width), 4 * width), 4 * width)
        grad_copies = [
            pltpu.make_async_copy(prompt_ref.at[:, columns], grads.at[pl.ds(0, count), :], grad_sems.at[0]),
            pltpu.make_async_copy(reply_ref.at[:, columns], grads.at[pl.ds(count, reply_ref.shape[0]), :], grad_sems.at[1]),
        ]
        if resume:
            grad_copies.append(pltpu.make_async_copy(earlier, total, total_sem.at[0]))
        if not project:
            copies += grad_copies
    pair_copies = []
    for slot in range(4):
        start = order_ref[slot] * width
        pair = []
        for side, chunk in enumerate((chunks[slot], chunks[4 + SWAPPED[slot]])):
            row = pl.multiple_of(start + (core if side == 0 else 1 - core) * size, size)
            pair.append(pltpu.make_async_copy(chunk, gathered.at[pl.ds(row, size), :], sems.at[slot, side]))
        pair_copies.append(pair)
        copies += pair
    if back and project:
        copies += grad_copies
    for copy in copies:
        copy.start()

    if project:
        for copy in row_copies:
            copy.wait()
        half = rows.shape[0] // 2
        across, along = head_ref[0] % 2, head_ref[0] // 2

        def upper(slot, side, dy):
            return pltpu.make_async_copy(held.at[slot, pl.ds(0, half), :], outs[side].at[dy], out_sems.at[slot, 0])

        def lower(slot, turn, dx):
            return pltpu.make_async_copy(held.at[slot, pl.ds(half, half), :], outs[2 + turn].at[dx], out_sems.at[slot, 1])

        def settle(slot):
            upper(slot, 0, 0).wait()
            lower(slot, 0, 0).wait()

        for slot in range(4):
            place, buffer = order_ref[slot], slot % 2
            if slot >= 2:
                settle(buffer)
            for copy in pair_copies[slot]:
                copy.wait()
            block = gathered[pl.ds(pl.multiple_of(place * width, width), width), :]
            held[buffer] = dot_nt(rows[...], block).astype(BF)
            target = half_ref[0] * 4 + place
            dy, dx = (target // 2 - along + 4) % 4, (target % 2 - across + 2) % 2
            for side in range(2):

                @pl.when(dx == side)
                def _():
                    upper(buffer, side, dy).start()

            for turn in range(4):

                @pl.when(dy == turn)
                def _():
                    lower(buffer, turn, dx).start()

    if back:
        for copy in grad_copies:
            copy.wait()
        for slot in range(4):
            if not project:
                for copy in pair_copies[slot]:
                    copy.wait()
            block = pl.ds(pl.multiple_of(order_ref[slot] * width, width), width)
            part = dot_nn(grads[:, block], gathered[block, :])
            if slot == 0 and not resume:
                total[...] = part
            else:
                total[...] += part
        if resume:
            count = ups[0].shape[0]
            ups[0][...] = total[:count, :].astype(BF)
            live = lax.broadcasted_iota(jnp.int32, ups[1].shape, 0) < length_ref[0]
            ups[1][...] = jnp.where(live, total[count:, :], 0.0).astype(BF)

    if project:
        settle(0)
        settle(1)


def absorb(scalars, chunks, att, grads, earlier=None, products=None):
    resume = earlier is not None or products is not None
    project, back = att is not None, grads is not None
    size, depth = chunks[0].shape
    width = 2 * size
    prompt_rows, reply_rows = (att or grads)[0].shape[0], (att or grads)[1].shape[0]
    total = prompt_rows + reply_rows
    anywhere = pl.BlockSpec(memory_space=pl.ANY)
    local = pl.BlockSpec(memory_space=pltpu.VMEM)
    scalar = pl.BlockSpec(memory_space=pltpu.SMEM)
    operands = [*chunks, *(att or ()), *(grads or ())]
    if back and resume:
        operands.append(earlier)
    aliases = {}
    out_specs, out_shape = [], []
    scratch = [pltpu.VMEM((8 * size, depth), BF), pltpu.SemaphoreType.DMA((4, 2))]
    if project:
        if resume:
            aliases = {len(scalars) + len(operands) + place: place for place in range(6)}
            operands += products
        out_specs += [anywhere] * 6
        out_shape += [jax.ShapeDtypeStruct((4, total // 2, width), BF)] * 2 + [jax.ShapeDtypeStruct((2, total // 2, width), BF)] * 4
        scratch += [
            pltpu.VMEM((total, depth), BF),
            pltpu.VMEM((2, total, width), BF),
            pltpu.SemaphoreType.DMA((2,)),
            pltpu.SemaphoreType.DMA((2, 2)),
        ]
    if back:
        scratch += [pltpu.VMEM((total, 8 * size), BF), pltpu.SemaphoreType.DMA((2,))]
        if resume:
            out_specs += [local] * 2
            out_shape += [jax.ShapeDtypeStruct((prompt_rows, depth), BF), jax.ShapeDtypeStruct((reply_rows, depth), BF)]
            scratch += [pltpu.VMEM((total, depth), F32), pltpu.SemaphoreType.DMA((1,))]
        else:
            out_specs.append(local)
            out_shape.append(jax.ShapeDtypeStruct((total, depth), F32))
    count = int(project) + int(back)
    return pl.pallas_call(
        functools.partial(absorb_kernel, project, back, resume),
        in_specs=[scalar] * len(scalars) + [anywhere] * len(operands),
        out_specs=out_specs,
        out_shape=out_shape,
        input_output_aliases=aliases,
        scratch_shapes=scratch,
        compiler_params=pltpu.CompilerParams(vmem_limit_bytes=VMEM_LIMIT),
        cost_estimate=pl.CostEstimate(flops=2 * total * depth * 8 * size * count, bytes_accessed=9 * 2**20, transcendentals=0),
        name="absorb_both" if count == 2 else "absorb_products" if project else "absorb_upstream",
    )(*scalars, *operands)


SWAPPED = (0, 2, 1, 3)


def seq_perm(move):
    pairs = []
    for x in range(2):
        for z in range(4):
            for core in range(2):
                to_x, to_z, to_core = move(x, z, core)
                pairs.append((x * 8 + z * 2 + core, (to_x % 2) * 8 + (to_z % 4) * 2 + to_core % 2))
    return pairs


ALONG = seq_perm(lambda x, z, core: (x, z + 1 - 2 * core, core))
AGAINST = seq_perm(lambda x, z, core: (x, z - 1 + 2 * core, core))
PEER = seq_perm(lambda x, z, core: (x + 1, z, core))
SIBLING = seq_perm(lambda x, z, core: (x, z, core + 1))


def head_perm(dy, dx):
    return [(y * 2 + x, ((y + dy) % 4) * 2 + (x + dx) % 2) for y in range(4) for x in range(2)]


def body(prompt_query, prompt_key, prompt_value, reply_query, reply_key, reply_value, lengths, out_weight, prompt_grad, reply_grad):
    prompt_rows = prompt_query.shape[0]
    n_seq = lax.axis_size("seq")
    seq, head = lax.axis_index("seq"), lax.axis_index("head")
    scalar = lambda value: value.reshape(1).astype(jnp.int32)
    x, z, core = seq // 8, (seq // 2) % 4, seq % 2
    order = jnp.stack([(z - (1 - 2 * core) * hop) % 4 for hop in (0, 1, -1, 2)]).astype(jnp.int32)
    core, near, other, head = scalar(core), scalar(x), scalar(1 - x), scalar(head)
    own = jnp.concatenate([prompt_key, prompt_value], 1)
    kv = lax.all_to_all(jnp.broadcast_to(own[None], (n_seq,) + own.shape), "seq", 0, 0).reshape(n_seq * prompt_rows, 2 * DIM)
    mine = out_weight.T
    send = lambda chunk, perm: lax.ppermute(chunk, "seq", perm)
    along, against, peer = [send(mine, perm) for perm in (ALONG, AGAINST, PEER)]
    along, against, peer, kv = lax.optimization_barrier((along, against, peer, kv))
    far, peer_along = send(along, ALONG), send(peer, ALONG)
    near_twins = [send(chunk, SIBLING) for chunk in (mine, along, against)]
    weights, prompt_weights, reply_att, prompt_att, inverse, prompt_inverse = attention_forward(
        scalar(seq), lengths, reply_query, prompt_query, kv, reply_key, reply_value
    )
    far, peer, peer_along, near_twins, reply_att = lax.optimization_barrier((far, peer, peer_along, near_twins, reply_att))
    near_chunks = [mine, along, against, far, *near_twins, send(far, SIBLING)]
    peer_against, peer_far = send(peer, AGAINST), send(peer_along, ALONG)
    peer_twins = [send(chunk, SIBLING) for chunk in (peer, peer_along)]
    att, grads = (prompt_att, reply_att), (prompt_grad, reply_grad)
    *products, partial = absorb((order, core, head, near, lengths), near_chunks, att, grads)
    partial, products, peer_against, peer_far = lax.optimization_barrier((partial, products, peer_against, peer_far))
    peer_twins = peer_twins + [send(chunk, SIBLING) for chunk in (peer_against, peer_far)]
    far_chunks = [peer, peer_along, peer_against, peer_far, *peer_twins]
    far_scalars = (order, core, head, other, lengths)
    kept, sent, *turns = absorb(far_scalars, far_chunks, att, None, None, products)
    came = lax.ppermute(sent, "head", head_perm(0, 1))
    turned = [lax.ppermute(turns[dy], "head", head_perm(dy, 0)) for dy in (1, 2, 3)]
    prompt_up, reply_up = absorb(far_scalars, far_chunks, None, grads, partial)
    query_grad, prompt_query_grad, kv_grad, reply_key_grad, reply_value_grad = attention_backward(
        weights, prompt_weights, inverse, prompt_inverse, reply_query, reply_up, reply_att, prompt_query, prompt_up, prompt_att, kv, reply_key, reply_value
    )
    first = [(kept[dy].astype(F32) + came[dy].astype(F32)).astype(BF) for dy in range(4)]
    second = turns[0].astype(F32) + turned[0].astype(F32) + turned[1].astype(F32) + turned[2].astype(F32)
    second = second.astype(BF)
    first, second, kv_grad = lax.optimization_barrier((first, (second[0], second[1]), kv_grad))
    first = [first[0]] + [lax.ppermute(first[dy], "head", head_perm(dy, 0)) for dy in (1, 2, 3)]
    second = second[0].astype(F32) + lax.ppermute(second[1], "head", head_perm(0, 1)).astype(F32)
    first = first[0].astype(F32) + first[1].astype(F32) + first[2].astype(F32) + first[3].astype(F32)
    first, second = first.astype(BF), second.astype(BF)
    terms = lax.all_to_all(kv_grad.reshape(n_seq, prompt_rows, 2 * DIM), "seq", 0, 0)
    kv_total = jnp.sum(terms.astype(F32), axis=0).astype(BF)
    return (
        first[:prompt_rows],
        jnp.concatenate([first[prompt_rows:], second], 0),
        prompt_query_grad,
        kv_total[:, :DIM],
        kv_total[:, DIM:],
        query_grad,
        reply_key_grad,
        reply_value_grad,
    )


def solution(mesh):
    cut = P("seq", "head")
    in_specs = (cut, cut, cut, cut, cut, cut, P("seq"), P("head", "seq"), P("seq", None), P("seq", None))
    return jax.shard_map(body, mesh=mesh, in_specs=in_specs, out_specs=(cut,) * 8, check_vma=False)
```

```python
import functools

import jax
import jax.numpy as jnp
from jax import lax
from jax.experimental import pallas as pl
from jax.experimental.pallas import tpu as pltpu
from jax.sharding import PartitionSpec as P

DIM = 128
BF = jnp.bfloat16
F32 = jnp.float32
SCALE = DIM**-0.5
EXP_SCALE = SCALE * 1.4426950408889634
PER = 2
VMEM_LIMIT = 60 * 1024 * 1024


def dot_nn(a, b):
    return lax.dot_general(a, b, (((1,), (0,)), ((), ())), preferred_element_type=F32)


def dot_nt(a, b):
    return lax.dot_general(a, b, (((1,), (1,)), ((), ())), preferred_element_type=F32)


def fold(part):
    while part.shape[0] > 8:
        half = part.shape[0] // 2
        part = jnp.maximum(part[:half], part[half:])
    return part


def forward_kernel(
    index_ref, length_ref, query_ref, prompt_query_ref, key_ref, value_ref, reply_key_ref, reply_value_ref,
    weight_ref, prompt_weight_ref, out_ref, prompt_out_ref, inverse_ref, prompt_inverse_ref, value_t, scores, stack,
):
    step = pl.program_id(0)
    heads = pl.num_programs(0) - 1
    prompt = key_ref.shape[0]
    rows = query_ref.shape[0]
    keys = prompt + rows
    prompt_rows = prompt_query_ref.shape[0]

    @pl.when(step == 0)
    def _():
        value_t[:DIM, :prompt] = value_ref[...].T
        value_t[:DIM, prompt:] = reply_value_ref[...].T
        value_t[DIM:, :] = jnp.ones((value_t.shape[0] - DIM, keys), BF)

    def raise_block(slot, block, lanes, shift, seen=None):
        part = scores[slot, block, lanes]
        if seen is not None:
            part = jnp.where(seen, part, -jnp.inf)
        return jnp.exp2(part * EXP_SCALE - shift).astype(BF)

    def divide(total):
        inverse = 1.0 / total[DIM : DIM + 1, :]
        return (total[:DIM, :] * inverse).T, jnp.broadcast_to(inverse, (DIM, rows)).T

    def score(slot):
        query = query_ref[:, slot * DIM : (slot + 1) * DIM]
        half = rows // 2
        upper = None
        for start in range(0, prompt, 256):
            part = dot_nt(key_ref[start : start + 256, :], query)
            scores[slot, start : start + 256, :] = part
            upper = fold(part) if upper is None else jnp.maximum(upper, fold(part))
        scores[slot, prompt : prompt + half, :] = dot_nt(reply_key_ref[:half], query)
        scores[slot, prompt + half :, half:] = dot_nt(reply_key_ref[half:], query[half:])
        return upper

    def weigh(slot, upper):
        seen = lax.broadcasted_iota(jnp.int32, (DIM, DIM), 0) <= lax.broadcasted_iota(jnp.int32, (DIM, DIM), 1)
        for tile in range(rows // DIM):
            lanes = slice(tile * DIM, (tile + 1) * DIM)
            full = prompt + tile * DIM
            top = jnp.maximum(upper[:, lanes], fold(jnp.where(seen, scores[slot, full : full + DIM, lanes], -jnp.inf)))
            for start in range(prompt, full, DIM):
                top = jnp.maximum(top, fold(scores[slot, start : start + DIM, lanes]))
            shift = jnp.max(top, axis=0, keepdims=True) * EXP_SCALE
            for start in range(0, full, DIM):
                block = slice(start, start + DIM)
                weight_ref[slot, block, lanes] = raise_block(slot, block, lanes, shift)
            block = slice(full, full + DIM)
            weight_ref[slot, block, lanes] = raise_block(slot, block, lanes, shift, seen)
            if full + DIM < keys:
                weight_ref[slot, full + DIM :, lanes] = jnp.zeros((keys - full - DIM, DIM), BF)

    def attend(slot):
        lanes = slice(slot * DIM, (slot + 1) * DIM)
        out, inverse = divide(dot_nn(value_t[...], weight_ref[slot]))
        live = lax.broadcasted_iota(jnp.int32, (rows, DIM), 0) < length_ref[0]
        out_ref[:, lanes] = jnp.where(live, out, 0.0).astype(BF)
        inverse_ref[:, lanes] = inverse

    @pl.when(step < heads)
    def _():
        upper = score(0)
        for slot in range(PER):
            following = score(slot + 1) if slot + 1 < PER else None
            weigh(slot, upper)
            attend(slot)
            upper = following

    @pl.when(step == heads)
    def _():
        for head in range(rows // prompt_rows):
            stack[head * prompt_rows : (head + 1) * prompt_rows, :] = prompt_query_ref[:, head * DIM : (head + 1) * DIM]
        scores[0, :prompt, :] = dot_nt(key_ref[...], stack[...])
        place = lax.broadcasted_iota(jnp.int32, (DIM, DIM), 1) % prompt_rows + index_ref[0] * prompt_rows
        for tile in range(rows // DIM):
            lanes = slice(tile * DIM, (tile + 1) * DIM)
            masks = [lax.broadcasted_iota(jnp.int32, (DIM, DIM), 0) + start <= place for start in range(0, prompt, DIM)]
            top = None
            for start, seen in zip(range(0, prompt, DIM), masks):
                part = fold(jnp.where(seen, scores[0, start : start + DIM, lanes], -jnp.inf))
                top = part if top is None else jnp.maximum(top, part)
            top = jnp.max(top, axis=0, keepdims=True)
            for start, seen in zip(range(0, prompt, DIM), masks):
                block = slice(start, start + DIM)
                prompt_weight_ref[block, lanes] = raise_block(0, block, lanes, top * EXP_SCALE, seen)
        out, inverse = divide(dot_nn(value_t[:, :prompt], prompt_weight_ref[...]))
        prompt_inverse_ref[...] = inverse
        out = out.astype(BF)
        for head in range(rows // prompt_rows):
            prompt_out_ref[:, head * DIM : (head + 1) * DIM] = out[head * prompt_rows : (head + 1) * prompt_rows, :]


def attention_forward(index, length, reply_query, prompt_query, kv, reply_key, reply_value):
    rows, columns = reply_query.shape
    prompt_rows = prompt_query.shape[0]
    heads = columns // DIM
    prompt = kv.shape[0]
    keys = prompt + rows
    steps = heads // PER
    last = steps - 1
    whole = lambda shape: pl.BlockSpec(shape, lambda g: (0, 0))
    return pl.pallas_call(
        forward_kernel,
        grid=(steps + 1,),
        in_specs=[
            pl.BlockSpec(memory_space=pltpu.SMEM),
            pl.BlockSpec(memory_space=pltpu.SMEM),
            pl.BlockSpec((rows, PER * DIM), lambda g: (0, jnp.minimum(g, last))),
            whole((prompt_rows, columns)),
            pl.BlockSpec((prompt, DIM), lambda g: (0, 0)),
            pl.BlockSpec((prompt, DIM), lambda g: (0, 1)),
            whole((rows, DIM)),
            whole((rows, DIM)),
        ],
        out_specs=[
            pl.BlockSpec((PER, keys, rows), lambda g: (jnp.minimum(g, last), 0, 0)),
            whole((prompt, rows)),
            pl.BlockSpec((rows, PER * DIM), lambda g: (0, jnp.minimum(g, last))),
            whole((prompt_rows, columns)),
            pl.BlockSpec((rows, PER * DIM), lambda g: (0, jnp.minimum(g, last))),
            whole((rows, DIM)),
        ],
        out_shape=[
            jax.ShapeDtypeStruct((heads, keys, rows), BF),
            jax.ShapeDtypeStruct((prompt, rows), BF),
            jax.ShapeDtypeStruct((rows, columns), BF),
            jax.ShapeDtypeStruct((prompt_rows, columns), BF),
            jax.ShapeDtypeStruct((rows, columns), F32),
            jax.ShapeDtypeStruct((rows, DIM), F32),
        ],
        scratch_shapes=[
            pltpu.VMEM((DIM + 16, keys), BF),
            pltpu.VMEM((PER, keys, rows), F32),
            pltpu.VMEM((rows, DIM), BF),
        ],
        compiler_params=pltpu.CompilerParams(vmem_limit_bytes=VMEM_LIMIT),
        cost_estimate=pl.CostEstimate(flops=4 * heads * keys * rows * DIM, bytes_accessed=18 * 2**20, transcendentals=heads * keys * rows),
        name="attention_forward",
    )(index, length, reply_query, prompt_query, kv, kv, reply_key, reply_value)


def backward_kernel(
    weight_ref, prompt_weight_ref, query_ref, grad_ref, out_ref, prompt_query_ref, prompt_grad_ref, prompt_out_ref,
    inverse_ref, prompt_inverse_ref, key_ref, value_ref, reply_key_ref, reply_value_ref,
    query_grad_ref, prompt_query_grad_ref, kv_grad_ref, reply_key_grad_ref, reply_value_grad_ref,
    key_t, score_grad, key_grad, value_grad, stack,
):
    step = pl.program_id(0)
    heads = pl.num_programs(0) - 1
    prompt = key_ref.shape[0]
    rows = query_ref.shape[0]
    keys = prompt + rows
    half = rows // 2
    prompt_rows = prompt_query_ref.shape[0]

    @pl.when(step == 0)
    def _():
        key_t[:, :prompt] = key_ref[...].T
        key_t[:, prompt:] = reply_key_ref[...].T
        key_grad[...] = jnp.zeros_like(key_grad)
        value_grad[...] = jnp.zeros_like(value_grad)
        score_grad[:, prompt + half :, :half] = jnp.zeros((PER, half, half), BF)

    def row_delta(grad, out):
        return jnp.sum((grad.astype(F32) * out.astype(F32)).T, axis=0, keepdims=True)

    def key_block(slot, weight, value, grad, query, delta, start, size, low):
        block = slice(start, start + size)
        slope = dot_nt(value, grad)
        part = (weight.astype(F32) * (slope - delta)).astype(BF)
        score_grad[slot, block, low:] = part
        key_grad[block, :] += dot_nn(part, query)
        value_grad[block, :] += dot_nn(weight, grad)

    @pl.when(step < heads)
    def _():
        items = []
        for slot in range(PER):
            lanes = slice(slot * DIM, (slot + 1) * DIM)
            query, grad = query_ref[:, lanes], (grad_ref[:, lanes].astype(F32) * inverse_ref[:, lanes]).astype(BF)
            items.append((slot, query, grad, row_delta(grad, out_ref[:, lanes])))
        whole = [(value_ref, start, start, 512) for start in range(0, prompt, 512)] + [(reply_value_ref, 0, prompt, half)]
        for low, blocks in ((0, whole), (half, [(reply_value_ref, half, prompt + half, half)])):
            queries = jnp.concatenate([query[low:] for _, query, _, _ in items], 0)
            grads = jnp.concatenate([grad[low:] for _, _, grad, _ in items], 0)
            for source, base, start, size in blocks:
                value = source[base : base + size, :]
                block = slice(start, start + size)
                parts, weights = [], []
                for slot, _, grad, delta in items:
                    weight = weight_ref[slot, block, low:]
                    part = (weight.astype(F32) * (dot_nt(value, grad[low:]) - delta[:, low:])).astype(BF)
                    score_grad[slot, block, low:] = part
                    parts.append(part)
                    weights.append(weight)
                key_grad[block, :] += dot_nn(jnp.concatenate(parts, 1), queries)
                value_grad[block, :] += dot_nn(jnp.concatenate(weights, 1), grads)
        for slot in range(PER):
            lanes = slice(slot * DIM, (slot + 1) * DIM)
            query_grad_ref[:, lanes] = (dot_nn(key_t[...], score_grad[slot]).T * SCALE).astype(BF)

    @pl.when(step == heads)
    def _():
        count = rows // prompt_rows
        for head in range(count):
            place, lanes = slice(head * prompt_rows, (head + 1) * prompt_rows), slice(head * DIM, (head + 1) * DIM)
            stack[0, place, :] = prompt_query_ref[:, lanes]
            stack[1, place, :] = prompt_grad_ref[:, lanes]
            stack[2, place, :] = prompt_out_ref[:, lanes]
        query, grad = stack[0], (stack[1].astype(F32) * prompt_inverse_ref[...]).astype(BF)
        delta = row_delta(grad, stack[2])
        for start in range(0, prompt, 512):
            key_block(0, prompt_weight_ref[start : start + 512, :], value_ref[start : start + 512, :], grad, query, delta, start, 512, 0)
        result = (dot_nn(key_t[:, :prompt], score_grad[0, :prompt, :]).T * SCALE).astype(BF)
        for head in range(count):
            prompt_query_grad_ref[:, head * DIM : (head + 1) * DIM] = result[head * prompt_rows : (head + 1) * prompt_rows, :]
        kv_grad_ref[:, :DIM] = (key_grad[:prompt, :] * SCALE).astype(BF)
        kv_grad_ref[:, DIM:] = value_grad[:prompt, :].astype(BF)
        reply_key_grad_ref[...] = (key_grad[prompt:, :] * SCALE).astype(BF)
        reply_value_grad_ref[...] = value_grad[prompt:, :].astype(BF)


def attention_backward(weights, prompt_weights, inverse, prompt_inverse, reply_query, reply_up, reply_att, prompt_query, prompt_up, prompt_att, kv, reply_key, reply_value):
    rows, columns = reply_query.shape
    prompt_rows = prompt_query.shape[0]
    heads = columns // DIM
    prompt = kv.shape[0]
    keys = prompt + rows
    steps = heads // PER
    last = steps - 1
    whole = lambda shape: pl.BlockSpec(shape, lambda g: (0, 0))
    column = pl.BlockSpec((rows, PER * DIM), lambda g: (0, jnp.minimum(g, last)))
    return pl.pallas_call(
        backward_kernel,
        grid=(steps + 1,),
        in_specs=[
            pl.BlockSpec((PER, keys, rows), lambda g: (jnp.minimum(g, last), 0, 0)),
            whole((prompt, rows)),
            column,
            column,
            column,
            whole((prompt_rows, columns)),
            whole((prompt_rows, columns)),
            whole((prompt_rows, columns)),
            column,
            whole((rows, DIM)),
            pl.BlockSpec((prompt, DIM), lambda g: (0, 0)),
            pl.BlockSpec((prompt, DIM), lambda g: (0, 1)),
            whole((rows, DIM)),
            whole((rows, DIM)),
        ],
        out_specs=[
            column,
            whole((prompt_rows, columns)),
            whole((prompt, 2 * DIM)),
            whole((rows, DIM)),
            whole((rows, DIM)),
        ],
        out_shape=[
            jax.ShapeDtypeStruct((rows, columns), BF),
            jax.ShapeDtypeStruct((prompt_rows, columns), BF),
            jax.ShapeDtypeStruct((prompt, 2 * DIM), BF),
            jax.ShapeDtypeStruct((rows, DIM), BF),
            jax.ShapeDtypeStruct((rows, DIM), BF),
        ],
        scratch_shapes=[
            pltpu.VMEM((DIM, keys), BF),
            pltpu.VMEM((PER, keys, rows), BF),
            pltpu.VMEM((keys, DIM), F32),
            pltpu.VMEM((keys, DIM), F32),
            pltpu.VMEM((3, rows, DIM), BF),
        ],
        compiler_params=pltpu.CompilerParams(vmem_limit_bytes=VMEM_LIMIT),
        cost_estimate=pl.CostEstimate(flops=8 * heads * keys * rows * DIM, bytes_accessed=18 * 2**20, transcendentals=0),
        name="attention_backward",
    )(weights, prompt_weights, reply_query, reply_up, reply_att, prompt_query, prompt_up, prompt_att, inverse, prompt_inverse, kv, kv, reply_key, reply_value)


def absorb_kernel(project, back, resume, order_ref, core_ref, head_ref, half_ref, length_ref, *refs):
    refs = list(refs)
    take = lambda count: [refs.pop(0) for _ in range(count)]
    chunks = take(8)
    sides = []
    if project:
        sides.append(take(2))
    if back:
        sides.append(take(2))
    (earlier,) = take(1) if back and resume else (None,)
    if project and resume:
        take(6)
    outs = take(6) if project else None
    ups = take(2 if resume else 1) if back else None
    gathered, sems = take(2)
    if project:
        rows, held, row_sems, out_sems = take(4)
    if back:
        grads, grad_sems = take(2)
        total, total_sem = take(2) if resume else (ups[0], None)
    size, core = chunks[0].shape[0], core_ref[0]
    width = 2 * size

    copies = []
    if project:
        prompt_ref, reply_ref = sides[0]
        count = prompt_ref.shape[0]
        row_copies = [
            pltpu.make_async_copy(prompt_ref, rows.at[pl.ds(0, count), :], row_sems.at[0]),
            pltpu.make_async_copy(reply_ref, rows.at[pl.ds(count, reply_ref.shape[0]), :], row_sems.at[1]),
        ]
        copies += row_copies
    if back:
        prompt_ref, reply_ref = sides[-1]
        count = prompt_ref.shape[0]
        columns = pl.ds(pl.multiple_of(half_ref[0] * (4 * width), 4 * width), 4 * width)
        grad_copies = [
            pltpu.make_async_copy(prompt_ref.at[:, columns], grads.at[pl.ds(0, count), :], grad_sems.at[0]),
            pltpu.make_async_copy(reply_ref.at[:, columns], grads.at[pl.ds(count, reply_ref.shape[0]), :], grad_sems.at[1]),
        ]
        if resume:
            grad_copies.append(pltpu.make_async_copy(earlier, total, total_sem.at[0]))
        if not project:
            copies += grad_copies
    pair_copies = []
    for slot in range(4):
        start = order_ref[slot] * width
        pair = []
        for side, chunk in enumerate((chunks[slot], chunks[4 + SWAPPED[slot]])):
            row = pl.multiple_of(start + (core if side == 0 else 1 - core) * size, size)
            pair.append(pltpu.make_async_copy(chunk, gathered.at[pl.ds(row, size), :], sems.at[slot, side]))
        pair_copies.append(pair)
        copies += pair
    if back and project:
        copies += grad_copies
    for copy in copies:
        copy.start()

    if project:
        for copy in row_copies:
            copy.wait()
        half = rows.shape[0] // 2
        across, along = head_ref[0] % 2, head_ref[0] // 2

        def upper(slot, side, dy):
            return pltpu.make_async_copy(held.at[slot, pl.ds(0, half), :], outs[side].at[dy], out_sems.at[slot, 0])

        def lower(slot, turn, dx):
            return pltpu.make_async_copy(held.at[slot, pl.ds(half, half), :], outs[2 + turn].at[dx], out_sems.at[slot, 1])

        def settle(slot):
            upper(slot, 0, 0).wait()
            lower(slot, 0, 0).wait()

        for slot in range(4):
            place, buffer = order_ref[slot], slot % 2
            if slot >= 2:
                settle(buffer)
            for copy in pair_copies[slot]:
                copy.wait()
            block = gathered[pl.ds(pl.multiple_of(place * width, width), width), :]
            held[buffer] = dot_nt(rows[...], block).astype(BF)
            target = half_ref[0] * 4 + place
            dy, dx = (target // 2 - along + 4) % 4, (target % 2 - across + 2) % 2
            for side in range(2):

                @pl.when(dx == side)
                def _():
                    upper(buffer, side, dy).start()

            for turn in range(4):

                @pl.when(dy == turn)
                def _():
                    lower(buffer, turn, dx).start()

    if back:
        for copy in grad_copies:
            copy.wait()
        for slot in range(4):
            if not project:
                for copy in pair_copies[slot]:
                    copy.wait()
            block = pl.ds(pl.multiple_of(order_ref[slot] * width, width), width)
            part = dot_nn(grads[:, block], gathered[block, :])
            if slot == 0 and not resume:
                total[...] = part
            else:
                total[...] += part
        if resume:
            count = ups[0].shape[0]
            ups[0][...] = total[:count, :].astype(BF)
            live = lax.broadcasted_iota(jnp.int32, ups[1].shape, 0) < length_ref[0]
            ups[1][...] = jnp.where(live, total[count:, :], 0.0).astype(BF)

    if project:
        settle(0)
        settle(1)


def absorb(scalars, chunks, att, grads, earlier=None, products=None):
    resume = earlier is not None or products is not None
    project, back = att is not None, grads is not None
    size, depth = chunks[0].shape
    width = 2 * size
    prompt_rows, reply_rows = (att or grads)[0].shape[0], (att or grads)[1].shape[0]
    total = prompt_rows + reply_rows
    anywhere = pl.BlockSpec(memory_space=pl.ANY)
    local = pl.BlockSpec(memory_space=pltpu.VMEM)
    scalar = pl.BlockSpec(memory_space=pltpu.SMEM)
    operands = [*chunks, *(att or ()), *(grads or ())]
    if back and resume:
        operands.append(earlier)
    aliases = {}
    out_specs, out_shape = [], []
    scratch = [pltpu.VMEM((8 * size, depth), BF), pltpu.SemaphoreType.DMA((4, 2))]
    if project:
        if resume:
            aliases = {len(scalars) + len(operands) + place: place for place in range(6)}
            operands += products
        out_specs += [anywhere] * 6
        out_shape += [jax.ShapeDtypeStruct((4, total // 2, width), BF)] * 2 + [jax.ShapeDtypeStruct((2, total // 2, width), BF)] * 4
        scratch += [
            pltpu.VMEM((total, depth), BF),
            pltpu.VMEM((2, total, width), BF),
            pltpu.SemaphoreType.DMA((2,)),
            pltpu.SemaphoreType.DMA((2, 2)),
        ]
    if back:
        scratch += [pltpu.VMEM((total, 8 * size), BF), pltpu.SemaphoreType.DMA((2,))]
        if resume:
            out_specs += [local] * 2
            out_shape += [jax.ShapeDtypeStruct((prompt_rows, depth), BF), jax.ShapeDtypeStruct((reply_rows, depth), BF)]
            scratch += [pltpu.VMEM((total, depth), F32), pltpu.SemaphoreType.DMA((1,))]
        else:
            out_specs.append(local)
            out_shape.append(jax.ShapeDtypeStruct((total, depth), F32))
    count = int(project) + int(back)
    return pl.pallas_call(
        functools.partial(absorb_kernel, project, back, resume),
        in_specs=[scalar] * len(scalars) + [anywhere] * len(operands),
        out_specs=out_specs,
        out_shape=out_shape,
        input_output_aliases=aliases,
        scratch_shapes=scratch,
        compiler_params=pltpu.CompilerParams(vmem_limit_bytes=VMEM_LIMIT),
        cost_estimate=pl.CostEstimate(flops=2 * total * depth * 8 * size * count, bytes_accessed=9 * 2**20, transcendentals=0),
        name="absorb_both" if count == 2 else "absorb_products" if project else "absorb_upstream",
    )(*scalars, *operands)


SWAPPED = (0, 2, 1, 3)


def seq_perm(move):
    pairs = []
    for x in range(2):
        for z in range(4):
            for core in range(2):
                to_x, to_z, to_core = move(x, z, core)
                pairs.append((x * 8 + z * 2 + core, (to_x % 2) * 8 + (to_z % 4) * 2 + to_core % 2))
    return pairs


ALONG = seq_perm(lambda x, z, core: (x, z + 1 - 2 * core, core))
AGAINST = seq_perm(lambda x, z, core: (x, z - 1 + 2 * core, core))
PEER = seq_perm(lambda x, z, core: (x + 1, z, core))
SIBLING = seq_perm(lambda x, z, core: (x, z, core + 1))


def head_perm(dy, dx):
    return [(y * 2 + x, ((y + dy) % 4) * 2 + (x + dx) % 2) for y in range(4) for x in range(2)]


def body(prompt_query, prompt_key, prompt_value, reply_query, reply_key, reply_value, lengths, out_weight, prompt_grad, reply_grad):
    prompt_rows = prompt_query.shape[0]
    n_seq = lax.axis_size("seq")
    seq, head = lax.axis_index("seq"), lax.axis_index("head")
    scalar = lambda value: value.reshape(1).astype(jnp.int32)
    x, z, core = seq // 8, (seq // 2) % 4, seq % 2
    order = jnp.stack([(z - (1 - 2 * core) * hop) % 4 for hop in (0, 1, -1, 2)]).astype(jnp.int32)
    core, near, other, head = scalar(core), scalar(x), scalar(1 - x), scalar(head)
    own = jnp.concatenate([prompt_key, prompt_value], 1)
    kv = lax.all_to_all(jnp.broadcast_to(own[None], (n_seq,) + own.shape), "seq", 0, 0).reshape(n_seq * prompt_rows, 2 * DIM)
    mine = out_weight.T
    send = lambda chunk, perm: lax.ppermute(chunk, "seq", perm)
    along, against, peer = [send(mine, perm) for perm in (ALONG, AGAINST, PEER)]
    along, against, peer, kv = lax.optimization_barrier((along, against, peer, kv))
    far, peer_along = send(along, ALONG), send(peer, ALONG)
    near_twins = [send(chunk, SIBLING) for chunk in (mine, along, against)]
    weights, prompt_weights, reply_att, prompt_att, inverse, prompt_inverse = attention_forward(
        scalar(seq), lengths, reply_query, prompt_query, kv, reply_key, reply_value
    )
    far, peer, peer_along, near_twins, reply_att = lax.optimization_barrier((far, peer, peer_along, near_twins, reply_att))
    near_chunks = [mine, along, against, far, *near_twins, send(far, SIBLING)]
    peer_against, peer_far = send(peer, AGAINST), send(peer_along, ALONG)
    peer_twins = [send(chunk, SIBLING) for chunk in (peer, peer_along)]
    att, grads = (prompt_att, reply_att), (prompt_grad, reply_grad)
    *products, partial = absorb((order, core, head, near, lengths), near_chunks, att, grads)
    partial, products, peer_against, peer_far = lax.optimization_barrier((partial, products, peer_against, peer_far))
    peer_twins = peer_twins + [send(chunk, SIBLING) for chunk in (peer_against, peer_far)]
    far_chunks = [peer, peer_along, peer_against, peer_far, *peer_twins]
    far_scalars = (order, core, head, other, lengths)
    kept, sent, *turns = absorb(far_scalars, far_chunks, att, None, None, products)
    came = lax.ppermute(sent, "head", head_perm(0, 1))
    turned = [lax.ppermute(turns[dy], "head", head_perm(dy, 0)) for dy in (1, 2, 3)]
    prompt_up, reply_up = absorb(far_scalars, far_chunks, None, grads, partial)
    query_grad, prompt_query_grad, kv_grad, reply_key_grad, reply_value_grad = attention_backward(
        weights, prompt_weights, inverse, prompt_inverse, reply_query, reply_up, reply_att, prompt_query, prompt_up, prompt_att, kv, reply_key, reply_value
    )
    first = [(kept[dy].astype(F32) + came[dy].astype(F32)).astype(BF) for dy in range(4)]
    second = turns[0].astype(F32) + turned[0].astype(F32) + turned[1].astype(F32) + turned[2].astype(F32)
    second = second.astype(BF)
    first, second, kv_grad = lax.optimization_barrier((first, (second[0], second[1]), kv_grad))
    first = [first[0]] + [lax.ppermute(first[dy], "head", head_perm(dy, 0)) for dy in (1, 2, 3)]
    second = second[0].astype(F32) + lax.ppermute(second[1], "head", head_perm(0, 1)).astype(F32)
    first = first[0].astype(F32) + first[1].astype(F32) + first[2].astype(F32) + first[3].astype(F32)
    first, second = first.astype(BF), second.astype(BF)
    terms = lax.all_to_all(kv_grad.reshape(n_seq, prompt_rows, 2 * DIM), "seq", 0, 0)
    kv_total = jnp.sum(terms.astype(F32), axis=0).astype(BF)
    return (
        first[:prompt_rows],
        jnp.concatenate([first[prompt_rows:], second], 0),
        prompt_query_grad,
        kv_total[:, :DIM],
        kv_total[:, DIM:],
        query_grad,
        reply_key_grad,
        reply_value_grad,
    )


def solution(mesh):
    cut = P("seq", "head")
    in_specs = (cut, cut, cut, cut, cut, cut, P("seq"), P("head", "seq"), P("seq", None), P("seq", None))
    return jax.shard_map(body, mesh=mesh, in_specs=in_specs, out_specs=(cut,) * 8, check_vma=False)
```

```python
import functools

import jax
import jax.numpy as jnp
from jax import lax
from jax.experimental import pallas as pl
from jax.experimental.pallas import tpu as pltpu
from jax.sharding import PartitionSpec as P

DIM = 128
BF = jnp.bfloat16
F32 = jnp.float32
SCALE = DIM**-0.5
EXP_SCALE = SCALE * 1.4426950408889634
PER = 2
VMEM_LIMIT = 60 * 1024 * 1024


def dot_nn(a, b):
    return lax.dot_general(a, b, (((1,), (0,)), ((), ())), preferred_element_type=F32)


def dot_nt(a, b):
    return lax.dot_general(a, b, (((1,), (1,)), ((), ())), preferred_element_type=F32)


def fold(part):
    while part.shape[0] > 8:
        half = part.shape[0] // 2
        part = jnp.maximum(part[:half], part[half:])
    return part


def forward_kernel(
    index_ref, length_ref, query_ref, prompt_query_ref, key_ref, value_ref, reply_key_ref, reply_value_ref,
    weight_ref, prompt_weight_ref, out_ref, prompt_out_ref, inverse_ref, prompt_inverse_ref, value_t, scores, stack,
):
    step = pl.program_id(0)
    heads = pl.num_programs(0) - 1
    prompt = key_ref.shape[0]
    rows = query_ref.shape[0]
    keys = prompt + rows
    prompt_rows = prompt_query_ref.shape[0]

    @pl.when(step == 0)
    def _():
        value_t[:DIM, :prompt] = value_ref[...].T
        value_t[:DIM, prompt:] = reply_value_ref[...].T
        value_t[DIM:, :] = jnp.ones((value_t.shape[0] - DIM, keys), BF)

    def raise_block(slot, block, lanes, shift, seen=None):
        part = scores[slot, block, lanes]
        if seen is not None:
            part = jnp.where(seen, part, -jnp.inf)
        return jnp.exp2(part * EXP_SCALE - shift).astype(BF)

    def divide(total):
        inverse = 1.0 / total[DIM : DIM + 1, :]
        return (total[:DIM, :] * inverse).T, jnp.broadcast_to(inverse, (DIM, rows)).T

    def score(slot):
        query = query_ref[:, slot * DIM : (slot + 1) * DIM]
        half = rows // 2
        upper = None
        for start in range(0, prompt, 256):
            part = dot_nt(key_ref[start : start + 256, :], query)
            scores[slot, start : start + 256, :] = part
            upper = fold(part) if upper is None else jnp.maximum(upper, fold(part))
        scores[slot, prompt : prompt + half, :] = dot_nt(reply_key_ref[:half], query)
        scores[slot, prompt + half :, half:] = dot_nt(reply_key_ref[half:], query[half:])
        return upper

    def weigh(slot, upper):
        seen = lax.broadcasted_iota(jnp.int32, (DIM, DIM), 0) <= lax.broadcasted_iota(jnp.int32, (DIM, DIM), 1)
        for tile in range(rows // DIM):
            lanes = slice(tile * DIM, (tile + 1) * DIM)
            full = prompt + tile * DIM
            top = jnp.maximum(upper[:, lanes], fold(jnp.where(seen, scores[slot, full : full + DIM, lanes], -jnp.inf)))
            for start in range(prompt, full, DIM):
                top = jnp.maximum(top, fold(scores[slot, start : start + DIM, lanes]))
            shift = jnp.max(top, axis=0, keepdims=True) * EXP_SCALE
            for start in range(0, full, DIM):
                block = slice(start, start + DIM)
                weight_ref[slot, block, lanes] = raise_block(slot, block, lanes, shift)
            block = slice(full, full + DIM)
            weight_ref[slot, block, lanes] = raise_block(slot, block, lanes, shift, seen)
            if full + DIM < keys:
                weight_ref[slot, full + DIM :, lanes] = jnp.zeros((keys - full - DIM, DIM), BF)

    def attend(slot):
        lanes = slice(slot * DIM, (slot + 1) * DIM)
        out, inverse = divide(dot_nn(value_t[...], weight_ref[slot]))
        live = lax.broadcasted_iota(jnp.int32, (rows, DIM), 0) < length_ref[0]
        out_ref[:, lanes] = jnp.where(live, out, 0.0).astype(BF)
        inverse_ref[:, lanes] = inverse

    @pl.when(step < heads)
    def _():
        upper = score(0)
        for slot in range(PER):
            following = score(slot + 1) if slot + 1 < PER else None
            weigh(slot, upper)
            attend(slot)
            upper = following

    @pl.when(step == heads)
    def _():
        for head in range(rows // prompt_rows):
            stack[head * prompt_rows : (head + 1) * prompt_rows, :] = prompt_query_ref[:, head * DIM : (head + 1) * DIM]
        scores[0, :prompt, :] = dot_nt(key_ref[...], stack[...])
        place = lax.broadcasted_iota(jnp.int32, (DIM, DIM), 1) % prompt_rows + index_ref[0] * prompt_rows
        for tile in range(rows // DIM):
            lanes = slice(tile * DIM, (tile + 1) * DIM)
            masks = [lax.broadcasted_iota(jnp.int32, (DIM, DIM), 0) + start <= place for start in range(0, prompt, DIM)]
            top = None
            for start, seen in zip(range(0, prompt, DIM), masks):
                part = fold(jnp.where(seen, scores[0, start : start + DIM, lanes], -jnp.inf))
                top = part if top is None else jnp.maximum(top, part)
            top = jnp.max(top, axis=0, keepdims=True)
            for start, seen in zip(range(0, prompt, DIM), masks):
                block = slice(start, start + DIM)
                prompt_weight_ref[block, lanes] = raise_block(0, block, lanes, top * EXP_SCALE, seen)
        out, inverse = divide(dot_nn(value_t[:, :prompt], prompt_weight_ref[...]))
        prompt_inverse_ref[...] = inverse
        out = out.astype(BF)
        for head in range(rows // prompt_rows):
            prompt_out_ref[:, head * DIM : (head + 1) * DIM] = out[head * prompt_rows : (head + 1) * prompt_rows, :]


def attention_forward(index, length, reply_query, prompt_query, kv, reply_key, reply_value):
    rows, columns = reply_query.shape
    prompt_rows = prompt_query.shape[0]
    heads = columns // DIM
    prompt = kv.shape[0]
    keys = prompt + rows
    steps = heads // PER
    last = steps - 1
    whole = lambda shape: pl.BlockSpec(shape, lambda g: (0, 0))
    return pl.pallas_call(
        forward_kernel,
        grid=(steps + 1,),
        in_specs=[
            pl.BlockSpec(memory_space=pltpu.SMEM),
            pl.BlockSpec(memory_space=pltpu.SMEM),
            pl.BlockSpec((rows, PER * DIM), lambda g: (0, jnp.minimum(g, last))),
            whole((prompt_rows, columns)),
            pl.BlockSpec((prompt, DIM), lambda g: (0, 0)),
            pl.BlockSpec((prompt, DIM), lambda g: (0, 1)),
            whole((rows, DIM)),
            whole((rows, DIM)),
        ],
        out_specs=[
            pl.BlockSpec((PER, keys, rows), lambda g: (jnp.minimum(g, last), 0, 0)),
            whole((prompt, rows)),
            pl.BlockSpec((rows, PER * DIM), lambda g: (0, jnp.minimum(g, last))),
            whole((prompt_rows, columns)),
            pl.BlockSpec((rows, PER * DIM), lambda g: (0, jnp.minimum(g, last))),
            whole((rows, DIM)),
        ],
        out_shape=[
            jax.ShapeDtypeStruct((heads, keys, rows), BF),
            jax.ShapeDtypeStruct((prompt, rows), BF),
            jax.ShapeDtypeStruct((rows, columns), BF),
            jax.ShapeDtypeStruct((prompt_rows, columns), BF),
            jax.ShapeDtypeStruct((rows, columns), F32),
            jax.ShapeDtypeStruct((rows, DIM), F32),
        ],
        scratch_shapes=[
            pltpu.VMEM((DIM + 16, keys), BF),
            pltpu.VMEM((PER, keys, rows), F32),
            pltpu.VMEM((rows, DIM), BF),
        ],
        compiler_params=pltpu.CompilerParams(vmem_limit_bytes=VMEM_LIMIT),
        cost_estimate=pl.CostEstimate(flops=4 * heads * keys * rows * DIM, bytes_accessed=18 * 2**20, transcendentals=heads * keys * rows),
        name="attention_forward",
    )(index, length, reply_query, prompt_query, kv, kv, reply_key, reply_value)


def backward_kernel(
    weight_ref, prompt_weight_ref, query_ref, grad_ref, out_ref, prompt_query_ref, prompt_grad_ref, prompt_out_ref,
    inverse_ref, prompt_inverse_ref, key_ref, value_ref, reply_key_ref, reply_value_ref,
    query_grad_ref, prompt_query_grad_ref, kv_grad_ref, reply_key_grad_ref, reply_value_grad_ref,
    key_t, score_grad, key_grad, value_grad, stack,
):
    step = pl.program_id(0)
    heads = pl.num_programs(0) - 1
    prompt = key_ref.shape[0]
    rows = query_ref.shape[0]
    keys = prompt + rows
    half = rows // 2
    prompt_rows = prompt_query_ref.shape[0]

    @pl.when(step == 0)
    def _():
        key_t[:, :prompt] = key_ref[...].T
        key_t[:, prompt:] = reply_key_ref[...].T
        key_grad[...] = jnp.zeros_like(key_grad)
        value_grad[...] = jnp.zeros_like(value_grad)
        score_grad[:, prompt + half :, :half] = jnp.zeros((PER, half, half), BF)

    def row_delta(grad, out):
        return jnp.sum((grad.astype(F32) * out.astype(F32)).T, axis=0, keepdims=True)

    def key_block(slot, weight, value, grad, query, delta, start, size, low):
        block = slice(start, start + size)
        slope = dot_nt(value, grad)
        part = (weight.astype(F32) * (slope - delta)).astype(BF)
        score_grad[slot, block, low:] = part
        key_grad[block, :] += dot_nn(part, query)
        value_grad[block, :] += dot_nn(weight, grad)

    @pl.when(step < heads)
    def _():
        items = []
        for slot in range(PER):
            lanes = slice(slot * DIM, (slot + 1) * DIM)
            query, grad = query_ref[:, lanes], (grad_ref[:, lanes].astype(F32) * inverse_ref[:, lanes]).astype(BF)
            items.append((slot, query, grad, row_delta(grad, out_ref[:, lanes])))
        whole = [(value_ref, start, start, 512) for start in range(0, prompt, 512)] + [(reply_value_ref, 0, prompt, half)]
        for low, blocks in ((0, whole), (half, [(reply_value_ref, half, prompt + half, half)])):
            queries = jnp.concatenate([query[low:] for _, query, _, _ in items], 0)
            grads = jnp.concatenate([grad[low:] for _, _, grad, _ in items], 0)
            for source, base, start, size in blocks:
                value = source[base : base + size, :]
                block = slice(start, start + size)
                parts, weights = [], []
                for slot, _, grad, delta in items:
                    weight = weight_ref[slot, block, low:]
                    part = (weight.astype(F32) * (dot_nt(value, grad[low:]) - delta[:, low:])).astype(BF)
                    score_grad[slot, block, low:] = part
                    parts.append(part)
                    weights.append(weight)
                key_grad[block, :] += dot_nn(jnp.concatenate(parts, 1), queries)
                value_grad[block, :] += dot_nn(jnp.concatenate(weights, 1), grads)
        for slot in range(PER):
            lanes = slice(slot * DIM, (slot + 1) * DIM)
            query_grad_ref[:, lanes] = (dot_nn(key_t[...], score_grad[slot]).T * SCALE).astype(BF)

    @pl.when(step == heads)
    def _():
        count = rows // prompt_rows
        for head in range(count):
            place, lanes = slice(head * prompt_rows, (head + 1) * prompt_rows), slice(head * DIM, (head + 1) * DIM)
            stack[0, place, :] = prompt_query_ref[:, lanes]
            stack[1, place, :] = prompt_grad_ref[:, lanes]
            stack[2, place, :] = prompt_out_ref[:, lanes]
        query, grad = stack[0], (stack[1].astype(F32) * prompt_inverse_ref[...]).astype(BF)
        delta = row_delta(grad, stack[2])
        for start in range(0, prompt, 512):
            key_block(0, prompt_weight_ref[start : start + 512, :], value_ref[start : start + 512, :], grad, query, delta, start, 512, 0)
        result = (dot_nn(key_t[:, :prompt], score_grad[0, :prompt, :]).T * SCALE).astype(BF)
        for head in range(count):
            prompt_query_grad_ref[:, head * DIM : (head + 1) * DIM] = result[head * prompt_rows : (head + 1) * prompt_rows, :]
        kv_grad_ref[:, :DIM] = (key_grad[:prompt, :] * SCALE).astype(BF)
        kv_grad_ref[:, DIM:] = value_grad[:prompt, :].astype(BF)
        reply_key_grad_ref[...] = (key_grad[prompt:, :] * SCALE).astype(BF)
        reply_value_grad_ref[...] = value_grad[prompt:, :].astype(BF)


def attention_backward(weights, prompt_weights, inverse, prompt_inverse, reply_query, reply_up, reply_att, prompt_query, prompt_up, prompt_att, kv, reply_key, reply_value):
    rows, columns = reply_query.shape
    prompt_rows = prompt_query.shape[0]
    heads = columns // DIM
    prompt = kv.shape[0]
    keys = prompt + rows
    steps = heads // PER
    last = steps - 1
    whole = lambda shape: pl.BlockSpec(shape, lambda g: (0, 0))
    column = pl.BlockSpec((rows, PER * DIM), lambda g: (0, jnp.minimum(g, last)))
    return pl.pallas_call(
        backward_kernel,
        grid=(steps + 1,),
        in_specs=[
            pl.BlockSpec((PER, keys, rows), lambda g: (jnp.minimum(g, last), 0, 0)),
            whole((prompt, rows)),
            column,
            column,
            column,
            whole((prompt_rows, columns)),
            whole((prompt_rows, columns)),
            whole((prompt_rows, columns)),
            column,
            whole((rows, DIM)),
            pl.BlockSpec((prompt, DIM), lambda g: (0, 0)),
            pl.BlockSpec((prompt, DIM), lambda g: (0, 1)),
            whole((rows, DIM)),
            whole((rows, DIM)),
        ],
        out_specs=[
            column,
            whole((prompt_rows, columns)),
            whole((prompt, 2 * DIM)),
            whole((rows, DIM)),
            whole((rows, DIM)),
        ],
        out_shape=[
            jax.ShapeDtypeStruct((rows, columns), BF),
            jax.ShapeDtypeStruct((prompt_rows, columns), BF),
            jax.ShapeDtypeStruct((prompt, 2 * DIM), BF),
            jax.ShapeDtypeStruct((rows, DIM), BF),
            jax.ShapeDtypeStruct((rows, DIM), BF),
        ],
        scratch_shapes=[
            pltpu.VMEM((DIM, keys), BF),
            pltpu.VMEM((PER, keys, rows), BF),
            pltpu.VMEM((keys, DIM), F32),
            pltpu.VMEM((keys, DIM), F32),
            pltpu.VMEM((3, rows, DIM), BF),
        ],
        compiler_params=pltpu.CompilerParams(vmem_limit_bytes=VMEM_LIMIT),
        cost_estimate=pl.CostEstimate(flops=8 * heads * keys * rows * DIM, bytes_accessed=18 * 2**20, transcendentals=0),
        name="attention_backward",
    )(weights, prompt_weights, reply_query, reply_up, reply_att, prompt_query, prompt_up, prompt_att, inverse, prompt_inverse, kv, kv, reply_key, reply_value)


def absorb_kernel(project, back, resume, order_ref, core_ref, head_ref, half_ref, length_ref, *refs):
    refs = list(refs)
    take = lambda count: [refs.pop(0) for _ in range(count)]
    chunks = take(8)
    sides = []
    if project:
        sides.append(take(2))
    if back:
        sides.append(take(2))
    (earlier,) = take(1) if back and resume else (None,)
    if project and resume:
        take(6)
    outs = take(6) if project else None
    ups = take(2 if resume else 1) if back else None
    gathered, sems = take(2)
    if project:
        rows, held, row_sems, out_sems = take(4)
    if back:
        grads, grad_sems = take(2)
        total, total_sem = take(2) if resume else (ups[0], None)
    size, core = chunks[0].shape[0], core_ref[0]
    width = 2 * size

    copies = []
    if project:
        prompt_ref, reply_ref = sides[0]
        count = prompt_ref.shape[0]
        row_copies = [
            pltpu.make_async_copy(prompt_ref, rows.at[pl.ds(0, count), :], row_sems.at[0]),
            pltpu.make_async_copy(reply_ref, rows.at[pl.ds(count, reply_ref.shape[0]), :], row_sems.at[1]),
        ]
        copies += row_copies
    if back:
        prompt_ref, reply_ref = sides[-1]
        count = prompt_ref.shape[0]
        columns = pl.ds(pl.multiple_of(half_ref[0] * (4 * width), 4 * width), 4 * width)
        grad_copies = [
            pltpu.make_async_copy(prompt_ref.at[:, columns], grads.at[pl.ds(0, count), :], grad_sems.at[0]),
            pltpu.make_async_copy(reply_ref.at[:, columns], grads.at[pl.ds(count, reply_ref.shape[0]), :], grad_sems.at[1]),
        ]
        if resume:
            grad_copies.append(pltpu.make_async_copy(earlier, total, total_sem.at[0]))
        if not project:
            copies += grad_copies
    pair_copies = []
    for slot in range(4):
        start = order_ref[slot] * width
        pair = []
        for side, chunk in enumerate((chunks[slot], chunks[4 + SWAPPED[slot]])):
            row = pl.multiple_of(start + (core if side == 0 else 1 - core) * size, size)
            pair.append(pltpu.make_async_copy(chunk, gathered.at[pl.ds(row, size), :], sems.at[slot, side]))
        pair_copies.append(pair)
        copies += pair
    if back and project:
        copies += grad_copies
    for copy in copies:
        copy.start()

    if project:
        for copy in row_copies:
            copy.wait()
        half = rows.shape[0] // 2
        across, along = head_ref[0] % 2, head_ref[0] // 2

        def upper(slot, side, dy):
            return pltpu.make_async_copy(held.at[slot, pl.ds(0, half), :], outs[side].at[dy], out_sems.at[slot, 0])

        def lower(slot, turn, dx):
            return pltpu.make_async_copy(held.at[slot, pl.ds(half, half), :], outs[2 + turn].at[dx], out_sems.at[slot, 1])

        def settle(slot):
            upper(slot, 0, 0).wait()
            lower(slot, 0, 0).wait()

        for slot in range(4):
            place, buffer = order_ref[slot], slot % 2
            if slot >= 2:
                settle(buffer)
            for copy in pair_copies[slot]:
                copy.wait()
            block = gathered[pl.ds(pl.multiple_of(place * width, width), width), :]
            held[buffer] = dot_nt(rows[...], block).astype(BF)
            target = half_ref[0] * 4 + place
            dy, dx = (target // 2 - along + 4) % 4, (target % 2 - across + 2) % 2
            for side in range(2):

                @pl.when(dx == side)
                def _():
                    upper(buffer, side, dy).start()

            for turn in range(4):

                @pl.when(dy == turn)
                def _():
                    lower(buffer, turn, dx).start()

    if back:
        for copy in grad_copies:
            copy.wait()
        for slot in range(4):
            if not project:
                for copy in pair_copies[slot]:
                    copy.wait()
            block = pl.ds(pl.multiple_of(order_ref[slot] * width, width), width)
            part = dot_nn(grads[:, block], gathered[block, :])
            if slot == 0 and not resume:
                total[...] = part
            else:
                total[...] += part
        if resume:
            count = ups[0].shape[0]
            ups[0][...] = total[:count, :].astype(BF)
            live = lax.broadcasted_iota(jnp.int32, ups[1].shape, 0) < length_ref[0]
            ups[1][...] = jnp.where(live, total[count:, :], 0.0).astype(BF)

    if project:
        settle(0)
        settle(1)


def absorb(scalars, chunks, att, grads, earlier=None, products=None):
    resume = earlier is not None or products is not None
    project, back = att is not None, grads is not None
    size, depth = chunks[0].shape
    width = 2 * size
    prompt_rows, reply_rows = (att or grads)[0].shape[0], (att or grads)[1].shape[0]
    total = prompt_rows + reply_rows
    anywhere = pl.BlockSpec(memory_space=pl.ANY)
    local = pl.BlockSpec(memory_space=pltpu.VMEM)
    scalar = pl.BlockSpec(memory_space=pltpu.SMEM)
    operands = [*chunks, *(att or ()), *(grads or ())]
    if back and resume:
        operands.append(earlier)
    aliases = {}
    out_specs, out_shape = [], []
    scratch = [pltpu.VMEM((8 * size, depth), BF), pltpu.SemaphoreType.DMA((4, 2))]
    if project:
        if resume:
            aliases = {len(scalars) + len(operands) + place: place for place in range(6)}
            operands += products
        out_specs += [anywhere] * 6
        out_shape += [jax.ShapeDtypeStruct((4, total // 2, width), BF)] * 2 + [jax.ShapeDtypeStruct((2, total // 2, width), BF)] * 4
        scratch += [
            pltpu.VMEM((total, depth), BF),
            pltpu.VMEM((2, total, width), BF),
            pltpu.SemaphoreType.DMA((2,)),
            pltpu.SemaphoreType.DMA((2, 2)),
        ]
    if back:
        scratch += [pltpu.VMEM((total, 8 * size), BF), pltpu.SemaphoreType.DMA((2,))]
        if resume:
            out_specs += [local] * 2
            out_shape += [jax.ShapeDtypeStruct((prompt_rows, depth), BF), jax.ShapeDtypeStruct((reply_rows, depth), BF)]
            scratch += [pltpu.VMEM((total, depth), F32), pltpu.SemaphoreType.DMA((1,))]
        else:
            out_specs.append(local)
            out_shape.append(jax.ShapeDtypeStruct((total, depth), F32))
    count = int(project) + int(back)
    return pl.pallas_call(
        functools.partial(absorb_kernel, project, back, resume),
        in_specs=[scalar] * len(scalars) + [anywhere] * len(operands),
        out_specs=out_specs,
        out_shape=out_shape,
        input_output_aliases=aliases,
        scratch_shapes=scratch,
        compiler_params=pltpu.CompilerParams(vmem_limit_bytes=VMEM_LIMIT),
        cost_estimate=pl.CostEstimate(flops=2 * total * depth * 8 * size * count, bytes_accessed=9 * 2**20, transcendentals=0),
        name="absorb_both" if count == 2 else "absorb_products" if project else "absorb_upstream",
    )(*scalars, *operands)


SWAPPED = (0, 2, 1, 3)


def seq_perm(move):
    pairs = []
    for x in range(2):
        for z in range(4):
            for core in range(2):
                to_x, to_z, to_core = move(x, z, core)
                pairs.append((x * 8 + z * 2 + core, (to_x % 2) * 8 + (to_z % 4) * 2 + to_core % 2))
    return pairs


ALONG = seq_perm(lambda x, z, core: (x, z + 1 - 2 * core, core))
AGAINST = seq_perm(lambda x, z, core: (x, z - 1 + 2 * core, core))
PEER = seq_perm(lambda x, z, core: (x + 1, z, core))
SIBLING = seq_perm(lambda x, z, core: (x, z, core + 1))


def head_perm(dy, dx):
    return [(y * 2 + x, ((y + dy) % 4) * 2 + (x + dx) % 2) for y in range(4) for x in range(2)]


def body(prompt_query, prompt_key, prompt_value, reply_query, reply_key, reply_value, lengths, out_weight, prompt_grad, reply_grad):
    prompt_rows = prompt_query.shape[0]
    n_seq = lax.axis_size("seq")
    seq, head = lax.axis_index("seq"), lax.axis_index("head")
    scalar = lambda value: value.reshape(1).astype(jnp.int32)
    x, z, core = seq // 8, (seq // 2) % 4, seq % 2
    order = jnp.stack([(z - (1 - 2 * core) * hop) % 4 for hop in (0, 1, -1, 2)]).astype(jnp.int32)
    core, near, other, head = scalar(core), scalar(x), scalar(1 - x), scalar(head)
    own = jnp.concatenate([prompt_key, prompt_value], 1)
    kv = lax.all_to_all(jnp.broadcast_to(own[None], (n_seq,) + own.shape), "seq", 0, 0).reshape(n_seq * prompt_rows, 2 * DIM)
    mine = out_weight.T
    send = lambda chunk, perm: lax.ppermute(chunk, "seq", perm)
    along, against, peer = [send(mine, perm) for perm in (ALONG, AGAINST, PEER)]
    along, against, peer, kv = lax.optimization_barrier((along, against, peer, kv))
    far, peer_along = send(along, ALONG), send(peer, ALONG)
    near_twins = [send(chunk, SIBLING) for chunk in (mine, along, against)]
    weights, prompt_weights, reply_att, prompt_att, inverse, prompt_inverse = attention_forward(
        scalar(seq), lengths, reply_query, prompt_query, kv, reply_key, reply_value
    )
    far, peer, peer_along, near_twins, reply_att = lax.optimization_barrier((far, peer, peer_along, near_twins, reply_att))
    near_chunks = [mine, along, against, far, *near_twins, send(far, SIBLING)]
    peer_against, peer_far = send(peer, AGAINST), send(peer_along, ALONG)
    peer_twins = [send(chunk, SIBLING) for chunk in (peer, peer_along)]
    att, grads = (prompt_att, reply_att), (prompt_grad, reply_grad)
    *products, partial = absorb((order, core, head, near, lengths), near_chunks, att, grads)
    partial, products, peer_against, peer_far = lax.optimization_barrier((partial, products, peer_against, peer_far))
    peer_twins = peer_twins + [send(chunk, SIBLING) for chunk in (peer_against, peer_far)]
    far_chunks = [peer, peer_along, peer_against, peer_far, *peer_twins]
    far_scalars = (order, core, head, other, lengths)
    kept, sent, *turns = absorb(far_scalars, far_chunks, att, None, None, products)
    came = lax.ppermute(sent, "head", head_perm(0, 1))
    turned = [lax.ppermute(turns[dy], "head", head_perm(dy, 0)) for dy in (1, 2, 3)]
    prompt_up, reply_up = absorb(far_scalars, far_chunks, None, grads, partial)
    query_grad, prompt_query_grad, kv_grad, reply_key_grad, reply_value_grad = attention_backward(
        weights, prompt_weights, inverse, prompt_inverse, reply_query, reply_up, reply_att, prompt_query, prompt_up, prompt_att, kv, reply_key, reply_value
    )
    first = [(kept[dy].astype(F32) + came[dy].astype(F32)).astype(BF) for dy in range(4)]
    first, kv_grad, own_turn = lax.optimization_barrier((first, kv_grad, turns[0]))
    second = own_turn.astype(F32) + turned[0].astype(F32) + turned[1].astype(F32) + turned[2].astype(F32)
    second = second.astype(BF)
    first = [first[0]] + [lax.ppermute(first[dy], "head", head_perm(dy, 0)) for dy in (1, 2, 3)]
    second = second[0].astype(F32) + lax.ppermute(second[1], "head", head_perm(0, 1)).astype(F32)
    first = first[0].astype(F32) + first[1].astype(F32) + first[2].astype(F32) + first[3].astype(F32)
    first, second = first.astype(BF), second.astype(BF)
    terms = lax.all_to_all(kv_grad.reshape(n_seq, prompt_rows, 2 * DIM), "seq", 0, 0)
    kv_total = jnp.sum(terms.astype(F32), axis=0).astype(BF)
    return (
        first[:prompt_rows],
        jnp.concatenate([first[prompt_rows:], second], 0),
        prompt_query_grad,
        kv_total[:, :DIM],
        kv_total[:, DIM:],
        query_grad,
        reply_key_grad,
        reply_value_grad,
    )


def solution(mesh):
    cut = P("seq", "head")
    in_specs = (cut, cut, cut, cut, cut, cut, P("seq"), P("head", "seq"), P("seq", None), P("seq", None))
    return jax.shard_map(body, mesh=mesh, in_specs=in_specs, out_specs=(cut,) * 8, check_vma=False)
```
